128 devices in a mesh: lat: 8 (over y, x_lo), lon: 16 (over z, x_hi, core).
Axes of the slice: x: 4 (x_hi: 2, x_lo: 2; x = x_hi * 2 + x_lo), y: 4, z: 4, core: 2. Of those that a mesh axis runs over, the one named last changes fastest.
Arguments:
- state: bfloat16 [76, 128, 4096], P(None, 'lat', 'lon'), may hold values from -6 to 6
- enc_weight: bfloat16 [76, 256], replicated, may hold values from -0.625 to 0.625
- kernels: float32 [2, 3, 3, 256], replicated, may hold values from -2 to 2
- gains: float32 [2, 256], replicated, may hold values from 0.5 to 2
- up_weight: bfloat16 [2, 256, 1024], replicated, may hold values from -0.375 to 0.375
- down_weight: bfloat16 [2, 1024, 256], replicated, may hold values from -0.1875 to 0.1875
- dec_weight: bfloat16 [256, 76], replicated, may hold values from -0.375 to 0.375
- obs_values: float32 [128, 128, 12, 76], P(('lat', 'lon')), may hold values from -6 to 6
- obs_cells: int32 [128, 128, 12], P(('lat', 'lon')), may hold values from 0 to 4095, as said below
- obs_depth: int32 [128, 128, 12], P(('lat', 'lon')), may hold values from 0 to 76, as said below
Outputs:
- gradient: float32 [76, 128, 4096], P(None, 'lat', 'lon')
The draws below stay inside these ranges and needn't reach their ends.
Inputs may be any that keep to these rules, and one draw needn't show every extreme that they name: `obs_cells`: A cell of the owner block, row-major over its 16 x 256 cells; cells may repeat. `obs_depth`: 0 marks an empty slot; the live slots of each source and owner come first; some owner receives 12 live profiles from every source.
All inputs are finite; a program needn't handle non-finite values.
Results may differ from the reference program's by a relative error of at most 0.017.
Values may be sent and summed in bfloat16 or wider, within the bound.
No kernel may reach another device: no remote copies, remote signals or barrier semaphores. Data moves between devices by JAX's collectives and lax.ppermute only.
A program may use at most 128 MiB of HBM per device.

```python
import math
import jax
import jax.numpy as jnp
from jax import lax

C_IN = 76
C_OUT = 76
HID = 256
EXP = 1024
BLOCKS = 2
LAT_DEV = 16
LON_DEV = 256
CAP = 12
NLAT = 128
NLON = 4096
CELLS_DEV = 4096
OWNERS = 128
N_LAT = 8
N_LON = 16


def owner_counts(key):
    heavy_key, pick_key, light_key = jax.random.split(key, 3)
    heavy_owner = jax.random.randint(heavy_key, (OWNERS,), 0, 4) == 0
    forced = jax.random.randint(pick_key, (), 0, OWNERS)
    heavy_owner = heavy_owner | (jnp.arange(OWNERS) == forced)
    light_count = jax.random.randint(light_key, (OWNERS, OWNERS), 1, CAP // 2 + 1)
    return jnp.where(heavy_owner[None, :], CAP, light_count)


def draw_obs_depth(key, part):
    counts = owner_counts(key)
    key = jax.random.fold_in(key, 7)
    levels_drawn = jax.random.randint(key, (OWNERS, OWNERS, CAP), 1, C_OUT + 1)
    in_use = jnp.arange(CAP)[None, None, :] < counts[:, :, None]
    return jnp.where(in_use, levels_drawn, 0).astype(jnp.int32)


def draw_obs_cells(key, part):
    key = jax.random.fold_in(key, 11)
    return jax.random.randint(key, (OWNERS, OWNERS, CAP), 0, CELLS_DEV).astype(jnp.int32)


def steps_of(key, dims, shards, least, high):
    def one(dim, parts):
        heights = jax.random.uniform(jax.random.fold_in(jax.random.fold_in(key, 6), dim), (parts,), jnp.float32, least / len(shards), high / len(shards))
        return jnp.repeat(jnp.exp(heights), dims[dim] // parts).reshape((-1,) + (1,) * (len(dims) - dim - 1))

    gain = one(*shards[0])
    for cut in shards[1:]:
        gain = gain * one(*cut)
    return gain


def scatter_about(stream_key, shape, deviation, most, pieces=(), held_as=jnp.bfloat16):
    loudness = steps_of(stream_key, shape, pieces, -0.22, 0.18) if pieces else 1.0
    result = jax.random.normal(stream_key, shape, jnp.float32) * deviation * loudness
    return jnp.minimum(jnp.maximum(result, -most), most).astype(held_as)


def setup_inputs(seed: int = 0) -> dict:
    seeds = jax.random.split(jax.random.key(seed), 11)
    return {
        "state": scatter_about(seeds[0], (C_IN, NLAT, NLON), 1.0, 6.0, ((1, 8), (2, 16))),
        "enc_weight": scatter_about(seeds[1], (C_IN, HID), C_IN ** -0.5, 0.625),
        "kernels": scatter_about(seeds[2], (BLOCKS, 3, 3, HID), 9 ** -0.5, 2.0, (), jnp.float32),
        "gains": jnp.clip(jnp.exp(jax.random.uniform(seeds[3], (BLOCKS, HID), jnp.float32, math.log(0.5), math.log(2.0))), 0.5, 2.0),
        "up_weight": scatter_about(seeds[4], (BLOCKS, HID, EXP), HID ** -0.5, 0.375),
        "down_weight": scatter_about(seeds[5], (BLOCKS, EXP, HID), EXP ** -0.5, 0.1875),
        "dec_weight": scatter_about(seeds[6], (HID, C_OUT), HID ** -0.5, 0.375),
        "obs_values": scatter_about(seeds[7], (OWNERS, OWNERS, CAP, C_OUT), 1.0, 6.0, ((0, 128),), jnp.float32),
        "obs_cells": draw_obs_cells(jax.random.fold_in(seeds[10], 71), 0),
        "obs_depth": draw_obs_depth(jax.random.fold_in(seeds[10], 71), 0),
    }


EPSILON = 1e-06
SQRT_TWO_PI = math.sqrt(2.0 / math.pi)

def gelu_tanh(inputs):
    cubic = inputs + 0.044715 * inputs * inputs * inputs
    return 0.5 * inputs * (1.0 + jnp.tanh(SQRT_TWO_PI * cubic))

def gelu_slope(inputs):
    tangent = jnp.tanh(SQRT_TWO_PI * (inputs + 0.044715 * inputs * inputs * inputs))
    return 0.5 * (1.0 + tangent) + 0.5 * inputs * (1.0 - tangent * tangent) * SQRT_TWO_PI * (1.0 + 3.0 * 0.044715 * inputs * inputs)

def depthwise(padded, kernel):
    height = padded.shape[0] - 2
    breadth = padded.shape[1] - 2
    summed = jnp.zeros((height, breadth, padded.shape[2]), jnp.float32)
    for row_off in range(3):
        for col_off in range(3):
            summed = summed + kernel[row_off, col_off] * padded[row_off:row_off + height, col_off:col_off + breadth].astype(jnp.float32)
    return summed

def pad_grid(grid_field):
    wrapped = jnp.concatenate([grid_field[:, -1:], grid_field, grid_field[:, :1]], axis=1)
    return jnp.pad(wrapped, ((1, 1), (0, 0), (0, 0)))

def normalize(spatial, gain_vec):
    inv_rms = lax.rsqrt(lax.optimization_barrier(jnp.mean(spatial * spatial, axis=-1, keepdims=True)) + EPSILON)
    return (inv_rms, (spatial * inv_rms * gain_vec).astype(jnp.bfloat16))

def norm_adjoint(grad_n, spatial, inv_rms, gain_vec):
    weighted = grad_n * gain_vec
    projection = lax.optimization_barrier(jnp.mean(weighted * spatial, axis=-1, keepdims=True))
    return (inv_rms * weighted - spatial * inv_rms * inv_rms * inv_rms * projection).astype(jnp.bfloat16)

def mlp_forward(normed, w_up, w_down):
    pre_act = jnp.dot(normed, w_up, preferred_element_type=jnp.float32)
    activated = gelu_tanh(pre_act).astype(jnp.bfloat16)
    return jnp.dot(activated, w_down, preferred_element_type=jnp.float32)

def mlp_adjoint(normed, grad_s, w_up, w_down):
    pre_act = jnp.dot(normed, w_up, preferred_element_type=jnp.float32)
    grad_g = jnp.dot(grad_s, w_down.T, preferred_element_type=jnp.float32)
    grad_p = (grad_g * gelu_slope(pre_act)).astype(jnp.bfloat16)
    return jnp.dot(grad_p, w_up.T, preferred_element_type=jnp.float32)

def reference(state, enc_weight, kernels, gains, up_weight, down_weight, dec_weight, obs_values, obs_cells, obs_depth):
    flat_state = state.reshape(C_IN, NLAT * NLON)
    hidden = lax.dot_general(flat_state, enc_weight, (((0,), (0,)), ((), ())), preferred_element_type=jnp.float32)
    hidden = hidden.astype(jnp.bfloat16).reshape(NLAT, NLON, HID)
    tape_list = []
    for block_id in range(BLOCKS):
        spatial = depthwise(pad_grid(hidden), kernels[block_id])
        inv_rms, normed = normalize(spatial, gains[block_id])
        w_up = up_weight[block_id]
        w_down = down_weight[block_id]
        branch = lax.map(lambda band_rows: mlp_forward(band_rows, w_up, w_down), normed.reshape(N_LAT, -1, HID))
        tape_list.append((spatial, inv_rms, normed))
        hidden = (hidden.astype(jnp.float32) + branch.reshape(NLAT, NLON, HID)).astype(jnp.bfloat16)
    output = jnp.dot(hidden.reshape(-1, HID), dec_weight, preferred_element_type=jnp.float32)
    blocks_view = output.reshape(N_LAT, LAT_DEV, N_LON, LON_DEV, C_OUT).transpose(0, 2, 1, 3, 4).reshape(OWNERS, CELLS_DEV, C_OUT)
    owner_ids = jnp.broadcast_to(jnp.arange(OWNERS, dtype=jnp.int32)[None, :, None], obs_cells.shape)
    sampled = blocks_view[owner_ids, obs_cells]
    level_mask = (jnp.arange(C_OUT, dtype=jnp.int32) < obs_depth[..., None]).astype(jnp.float32)
    misfit = (sampled - obs_values) * level_mask
    adjoint_blocks = jnp.zeros((OWNERS, CELLS_DEV, C_OUT), jnp.float32).at[owner_ids, obs_cells].add(misfit)
    adjoint_y = adjoint_blocks.reshape(N_LAT, N_LON, LAT_DEV, LON_DEV, C_OUT).transpose(0, 2, 1, 3, 4).reshape(NLAT * NLON, C_OUT).astype(jnp.bfloat16)
    grad_h = jnp.dot(adjoint_y, dec_weight.T, preferred_element_type=jnp.float32).reshape(NLAT, NLON, HID)
    for block_id in reversed(range(BLOCKS)):
        spatial, inv_rms, normed = tape_list[block_id]
        w_up = up_weight[block_id]
        w_down = down_weight[block_id]
        grad_s = grad_h.astype(jnp.bfloat16)
        grad_n = lax.map(lambda operands: mlp_adjoint(operands[0], operands[1], w_up, w_down), (normed.reshape(N_LAT, -1, HID), grad_s.reshape(N_LAT, -1, HID)))
        grad_d = norm_adjoint(grad_n.reshape(NLAT, NLON, HID), spatial, inv_rms, gains[block_id])
        grad_h = grad_h + depthwise(pad_grid(grad_d), kernels[block_id][::-1, ::-1])
    grad_zero = grad_h.astype(jnp.bfloat16).reshape(-1, HID)
    gradient = lax.dot_general(enc_weight, grad_zero, (((1,), (1,)), ((), ())), preferred_element_type=jnp.float32)
    return gradient.reshape(C_IN, NLAT, NLON)
```

```python
import functools
import math

import jax
import jax.numpy as jnp
from jax import lax
from jax.experimental import pallas as pl
from jax.experimental.pallas import tpu as pltpu
from jax.sharding import PartitionSpec as P

EPSILON = 1e-06
SQRT_TWO_PI = math.sqrt(2.0 / math.pi)
CUBIC = 0.044715
BF = jnp.bfloat16
F32 = jnp.float32

LAT = 16
LON = 256
HID = 256
EXP = 1024
LANES = 128
SIDE = 8
WIDE = LON + 2 * SIDE
HALO = 4
STEP = 2
CHUNK = 256
VMEM_LIMIT = 60 * 1024 * 1024
GELU_TYPE = BF


def whole(shape):
    return pl.BlockSpec(shape, lambda *_: (0,) * len(shape))


def rows_of(width, offset=0):
    return pl.BlockSpec((STEP, WIDE, width), lambda s, *_: (s + offset, 0, 0))


def params():
    return pltpu.CompilerParams(
        dimension_semantics=("arbitrary",), vmem_limit_bytes=VMEM_LIMIT
    )


def convolve(rows, kernel):
    out = []
    for r in range(len(rows) - 2):
        cols = []
        for e in range(3):
            cols.append(
                kernel[e] * rows[r] + kernel[3 + e] * rows[r + 1] + kernel[6 + e] * rows[r + 2]
            )
        out.append(cols[1] + pltpu.roll(cols[0], 1, 0) + pltpu.roll(cols[2], WIDE - 1, 0))
    return out


def taps(kernel_ref, flip):
    order = range(8, -1, -1) if flip else range(9)
    return [kernel_ref[t : t + 1, :] for t in order]


def gelu_pair(pre):
    v = pre.astype(GELU_TYPE)
    u = v * v
    t = jnp.tanh(v * (u * (SQRT_TWO_PI * CUBIC) + SQRT_TWO_PI))
    w = 1.0 + t
    doubled = v * w
    slope = w * (1.0 + (v * (u * (3.0 * SQRT_TWO_PI * CUBIC) + SQRT_TWO_PI)) * (1.0 - t))
    return doubled.astype(BF), slope.astype(BF)


def forward_rows(rows, center, kernel_ref, gain_ref, up_ref, down_ref, tape_ref, hat_ref, inv_ref):
    spatial = jnp.concatenate(convolve(rows, taps(kernel_ref, False)), axis=0)
    inv = lax.rsqrt(jnp.mean(spatial * spatial, axis=-1, keepdims=True) + EPSILON)
    hat = spatial * inv
    hat_ref[...] = hat.astype(BF).reshape(hat_ref.shape)
    inv_ref[...] = jnp.broadcast_to(inv, (inv.shape[0], LANES)).reshape(inv_ref.shape)
    normed = (hat * gain_ref[...]).astype(BF)
    total = center
    for j in range(EXP // CHUNK):
        cut = slice(j * CHUNK, (j + 1) * CHUNK)
        pre = jnp.dot(normed, up_ref[:, cut], preferred_element_type=F32)
        act, slope = gelu_pair(pre)
        tape_ref[:, :, cut] = slope.reshape(STEP, WIDE, CHUNK)
        total = total + jnp.dot(act, down_ref[cut, :], preferred_element_type=F32)
    return total


def row_mask(lat_ref, first):
    row = lat_ref[0] * LAT + first + pl.program_id(0) * STEP
    inside = []
    for r in range(STEP):
        ok = jnp.logical_and(row + r >= 0, row + r < lat_ref[1])
        inside.append(jnp.where(ok, 1.0, 0.0).astype(F32))
    return inside


def masked(values, inside):
    return jnp.stack([values[r * WIDE : (r + 1) * WIDE] * inside[r] for r in range(STEP)])


def forward_zero(
    lat_ref, left_ref, main_ref, right_ref, kernel_ref, gain_ref, up_ref, down_ref,
    out_ref, tape_ref, hat_ref, inv_ref,
):
    base = pl.program_id(0) * STEP
    rows = [
        jnp.concatenate(
            [
                left_ref[base + r].astype(F32),
                main_ref[base + r].astype(F32),
                right_ref[base + r].astype(F32),
            ],
            axis=0,
        )
        for r in range(STEP + 2)
    ]
    center = jnp.concatenate(rows[1:-1], axis=0)
    total = forward_rows(
        rows, center, kernel_ref, gain_ref, up_ref, down_ref, tape_ref, hat_ref, inv_ref
    )
    out_ref[...] = masked(total, row_mask(lat_ref, 1 - HALO)).astype(BF)


def forward_one(
    hidden_ref, kernel_ref, gain_ref, up_ref, down_ref, out_ref, tape_ref, hat_ref, inv_ref
):
    base = pl.program_id(0) * STEP
    rows = [hidden_ref[base + r].astype(F32) for r in range(STEP + 2)]
    center = jnp.concatenate(rows[1:-1], axis=0)
    total = forward_rows(
        rows, center, kernel_ref, gain_ref, up_ref, down_ref, tape_ref, hat_ref, inv_ref
    )
    out_ref[...] = total.astype(BF).reshape(out_ref.shape)


def mixed_adjoint(grad, gain_ref, up_ref, down_ref, tape_ref, hat_ref, inv_ref):
    grad_s = grad.astype(BF)
    grad_n = jnp.zeros((STEP * WIDE, HID), F32)
    for j in range(EXP // CHUNK):
        cut = slice(j * CHUNK, (j + 1) * CHUNK)
        grad_g = lax.dot_general(
            grad_s, down_ref[cut, :], (((1,), (1,)), ((), ())), preferred_element_type=F32
        )
        slope = tape_ref[:, :, cut].reshape(STEP * WIDE, CHUNK)
        grad_p = (grad_g * slope.astype(F32)).astype(BF)
        grad_n = grad_n + lax.dot_general(
            grad_p, up_ref[:, cut], (((1,), (1,)), ((), ())), preferred_element_type=F32
        )
    weighted = grad_n * gain_ref[...]
    hat = hat_ref[...].reshape(STEP * WIDE, HID).astype(F32)
    projection = jnp.mean(weighted * hat, axis=-1, keepdims=True)
    inv = inv_ref[...].reshape(STEP * WIDE, LANES)
    return jnp.concatenate([inv, inv], axis=1) * (weighted - hat * projection)


def adjoint_one(
    hidden_ref, left_ref, main_ref, right_ref, dec_ref, gain_ref, up_ref, down_ref,
    tape_ref, hat_ref, inv_ref, out_ref, adj_ref,
):
    hidden = hidden_ref[...].reshape(STEP * WIDE, HID)
    model = jnp.dot(hidden, dec_ref[...], preferred_element_type=F32)
    field = []
    for r in range(STEP):
        field += [left_ref[r], main_ref[r], right_ref[r]]
    field = jnp.concatenate(field, axis=0)
    adjoint = (field[:, LANES:] * model - field[:, :LANES]).astype(BF)
    adj_ref[...] = adjoint.reshape(adj_ref.shape)
    grad = lax.dot_general(
        adjoint, dec_ref[...], (((1,), (1,)), ((), ())), preferred_element_type=F32
    )
    grad_d = mixed_adjoint(grad, gain_ref, up_ref, down_ref, tape_ref, hat_ref, inv_ref)
    out_ref[...] = grad_d.astype(BF).reshape(out_ref.shape)


def adjoint_zero(
    lat_ref, above_ref, adj_ref, dec_ref, kernel_ref, gain_ref, up_ref, down_ref,
    tape_ref, hat_ref, inv_ref, out_ref, grad_ref,
):
    base = pl.program_id(0) * STEP
    rows = [above_ref[base + r].astype(F32) for r in range(STEP + 2)]
    grad = jnp.concatenate(convolve(rows, taps(kernel_ref, True)), axis=0)
    adjoint = jnp.concatenate([adj_ref[base + 1 + r] for r in range(STEP)], axis=0)
    grad = grad + lax.dot_general(
        adjoint, dec_ref[...], (((1,), (1,)), ((), ())), preferred_element_type=F32
    )
    grad_ref[...] = grad.astype(BF).reshape(grad_ref.shape)
    grad_d = mixed_adjoint(grad, gain_ref, up_ref, down_ref, tape_ref, hat_ref, inv_ref)
    out_ref[...] = masked(grad_d, row_mask(lat_ref, -1)).astype(BF)


def finish(above_ref, grad_ref, kernel_ref, enc_ref, out_ref):
    base = pl.program_id(0) * 8
    for r in range(8):
        rows = [above_ref[base + r + a].astype(F32) for a in range(3)]
        conv = convolve(rows, taps(kernel_ref, True))[0]
        grad = (conv + grad_ref[base + 1 + r].astype(F32))[SIDE : SIDE + LON].astype(BF)
        out_ref[:, r, :] = lax.dot_general(
            enc_ref[...], grad, (((1,), (1,)), ((), ())), preferred_element_type=F32
        )


def place_observations(levels, table_ref, out_ref, hot_ref, row_ref, value_ref):
    @pl.when(pl.program_id(0) == 0)
    def _():
        table = table_ref[...]
        flipped = jnp.transpose(table.astype(F32))
        slots = flipped.shape[1]
        column = flipped[levels + 1 : levels + 2, :]
        iota = lax.broadcasted_iota(jnp.int32, (LON, slots), 0).astype(F32)
        hot_ref[...] = jnp.where(iota == column, 1.0, 0.0).astype(BF)
        row_ref[...] = jnp.broadcast_to(flipped[levels : levels + 1, :], (16, slots))
        depth = table[:, levels + 2 : levels + 3].astype(F32)
        lane = lax.broadcasted_iota(jnp.int32, table.shape, 1)
        mask = jnp.where(lane.astype(F32) < depth, 1.0, 0.0)
        value_ref[:, :LANES] = (table.astype(F32) * mask).astype(BF)
        value_ref[:, LANES:] = mask.astype(BF)

    here = pl.program_id(0).astype(F32)
    keep = jnp.where(row_ref[0:1, :] == here, 1.0, 0.0).astype(BF)
    out_ref[0] = jnp.dot(hot_ref[...] * keep, value_ref[...], preferred_element_type=F32)


def pair_shift(low, high, axis, wrap):
    peers = lax.axis_size(axis)
    up = [(i, (i + 1) % peers) for i in range(peers if wrap else peers - 1)]
    down = [(j, i) for i, j in up]
    return lax.ppermute(high, axis, up), lax.ppermute(low, axis, down)


def cost(rows, dots, extra=0):
    return pl.CostEstimate(
        flops=2 * rows * WIDE * HID * EXP * dots + extra,
        bytes_accessed=rows * WIDE * EXP * 2,
        transcendentals=0,
    )


def sds(shape, dtype):
    return jax.ShapeDtypeStruct(shape, dtype)


def body(
    state, enc_weight, kernels, gains, up_weight, down_weight, dec_weight,
    obs_values, obs_cells, obs_depth,
):
    channels = state.shape[0]
    levels = dec_weight.shape[1]
    owners, slots = obs_cells.shape[1:]
    taps_flat = kernels.reshape(2, 9, HID)
    half_down = (down_weight.astype(F32) * 0.5).astype(BF)
    gain_rows = gains.reshape(2, 1, HID)
    dec = jnp.pad(dec_weight, ((0, 0), (0, LANES - levels)))
    lat = jnp.stack([lax.axis_index("lat"), lax.axis_size("lat") * LAT]).astype(jnp.int32)

    cells = obs_cells[0]
    tags = jnp.stack([cells // LON, cells % LON, obs_depth[0]], axis=-1).astype(BF)
    packed = jnp.concatenate([obs_values[0].astype(BF), tags], axis=-1)
    packed = jnp.pad(packed, ((0, 0), (0, 16 - slots), (0, LANES - levels - 3)))
    table = lax.all_to_all(packed, ("lat", "lon"), split_axis=0, concat_axis=0, tiled=True)

    top, bottom = pair_shift(state[:, :HALO], state[:, LAT - HALO :], "lat", False)
    tall = jnp.concatenate([top, state, bottom], axis=1)
    main = lax.dot_general(
        tall, enc_weight, (((0,), (0,)), ((), ())), preferred_element_type=F32
    ).astype(BF)
    left, right = pair_shift(main[:, :SIDE], main[:, LON - SIDE :], "lon", True)

    high0 = LAT + 2 * HALO - 2
    block = lambda b: (taps_flat[b], gain_rows[b], up_weight[b], half_down[b])
    block_specs = [whole((9, HID)), whole((1, HID)), whole((HID, EXP)), whole((EXP, HID))]

    def forward_outs(high):
        return (
            [
                sds((high, WIDE, HID), BF),
                sds((high, WIDE, EXP), BF),
                sds((high, WIDE, HID), BF),
                sds((high, WIDE, LANES), F32),
            ],
            [rows_of(HID), rows_of(EXP), rows_of(HID), rows_of(LANES)],
        )

    shapes, specs = forward_outs(high0)
    hidden, tape0, hat0, inv0 = pl.pallas_call(
        forward_zero,
        out_shape=shapes,
        grid_spec=pltpu.PrefetchScalarGridSpec(
            num_scalar_prefetch=1,
            grid=(high0 // STEP,),
            in_specs=[whole(left.shape), whole(main.shape), whole(right.shape)] + block_specs,
            out_specs=specs,
        ),
        compiler_params=params(),
        cost_estimate=cost(high0, 2),
        name="forward_zero",
    )(lat, left, main, right, *block(0))

    table = table.reshape(owners * 16, LANES)
    field = pl.pallas_call(
        functools.partial(place_observations, levels),
        out_shape=sds((LAT, LON, 2 * LANES), F32),
        grid=(LAT,),
        in_specs=[whole(table.shape)],
        out_specs=pl.BlockSpec((1, LON, 2 * LANES), lambda s: (s, 0, 0)),
        scratch_shapes=[
            pltpu.VMEM((LON, owners * 16), BF),
            pltpu.VMEM((16, owners * 16), F32),
            pltpu.VMEM((owners * 16, 2 * LANES), BF),
        ],
        compiler_params=params(),
        cost_estimate=pl.CostEstimate(
            flops=2 * LAT * LON * owners * 16 * 256, bytes_accessed=2**22, transcendentals=0
        ),
        name="place_observations",
    )(table)
    f_top, f_bottom = pair_shift(field[:2], field[LAT - 2 :], "lat", False)
    field = jnp.concatenate([f_top, field, f_bottom], axis=0)
    f_left, f_right = pair_shift(field[:, :SIDE], field[:, LON - SIDE :], "lon", True)

    high1 = high0 - 2
    shapes, specs = forward_outs(high1)
    final, tape1, hat1, inv1 = pl.pallas_call(
        forward_one,
        out_shape=shapes,
        grid=(high1 // STEP,),
        in_specs=[whole(hidden.shape)] + block_specs,
        out_specs=specs,
        compiler_params=params(),
        cost_estimate=cost(high1, 2),
        name="forward_one",
    )(hidden, *block(1))

    side = pl.BlockSpec((STEP, SIDE, 2 * LANES), lambda s: (s, 0, 0))
    centre = pl.BlockSpec((STEP, LON, 2 * LANES), lambda s: (s, 0, 0))
    tap, gain, up, down = block(1)
    grad_d1, adjoint = pl.pallas_call(
        adjoint_one,
        out_shape=[sds((high1, WIDE, HID), BF), sds((high1, WIDE, LANES), BF)],
        grid=(high1 // STEP,),
        in_specs=[rows_of(HID), side, centre, side, whole(dec.shape)]
        + block_specs[1:]
        + [rows_of(EXP), rows_of(HID), rows_of(LANES)],
        out_specs=[rows_of(HID), rows_of(LANES)],
        compiler_params=params(),
        cost_estimate=cost(high1, 2),
        name="adjoint_one",
    )(final, f_left, field, f_right, dec, gain, up, down, tape1, hat1, inv1)

    high2 = high1 - 2
    _, gain, up, down = block(0)
    grad_d0, grad1 = pl.pallas_call(
        adjoint_zero,
        out_shape=[sds((high2, WIDE, HID), BF), sds((high2, WIDE, HID), BF)],
        grid_spec=pltpu.PrefetchScalarGridSpec(
            num_scalar_prefetch=1,
            grid=(high2 // STEP,),
            in_specs=[whole(grad_d1.shape), whole(adjoint.shape), whole(dec.shape)]
            + block_specs
            + [rows_of(EXP, 1), rows_of(HID, 1), rows_of(LANES, 1)],
            out_specs=[rows_of(HID), rows_of(HID)],
        ),
        compiler_params=params(),
        cost_estimate=cost(high2, 2),
        name="adjoint_zero",
    )(lat, grad_d1, adjoint, dec, tap, gain, up, down, tape0, hat0, inv0)

    return pl.pallas_call(
        finish,
        out_shape=sds((channels, LAT, LON), F32),
        grid=(LAT // 8,),
        in_specs=[
            whole(grad_d0.shape),
            whole(grad1.shape),
            whole((9, HID)),
            whole((channels, HID)),
        ],
        out_specs=pl.BlockSpec((channels, 8, LON), lambda s: (0, s, 0)),
        compiler_params=params(),
        cost_estimate=cost(2, 1),
        name="finish",
    )(grad_d0, grad1, taps_flat[0], enc_weight)


def solution(mesh):
    in_specs = (
        P(None, "lat", "lon"),
        P(),
        P(),
        P(),
        P(),
        P(),
        P(),
        P(("lat", "lon"), None, None, None),
        P(("lat", "lon"), None, None),
        P(("lat", "lon"), None, None),
    )
    out_specs = P(None, "lat", "lon")
    return jax.shard_map(body, mesh=mesh, in_specs=in_specs, out_specs=out_specs, check_vma=False)
```

```python
import functools
import math

import jax
import jax.numpy as jnp
from jax import lax
from jax.experimental import pallas as pl
from jax.experimental.pallas import tpu as pltpu
from jax.sharding import PartitionSpec as P

EPSILON = 1e-06
SQRT_TWO_PI = math.sqrt(2.0 / math.pi)
CUBIC = SQRT_TWO_PI * 0.044715
BF = jnp.bfloat16
F32 = jnp.float32

LAT = 16
LON = 256
HID = 256
EXP = 1024
LANES = 128
SIDE = 8
WIDE = LON + 2 * SIDE
SUBL = 16
COLS = WIDE // SUBL
HALO = 4
R = 2
M = R * WIDE
CHUNK = 256
HIGH0 = LAT + 2 * HALO - 2
HIGH1 = HIGH0 - 2
HIGH2 = HIGH1 - 2
TAPE = HIGH2 * WIDE


def sds(shape, dtype):
    return jax.ShapeDtypeStruct(shape, dtype)


def vmem():
    return pl.BlockSpec(memory_space=pltpu.VMEM)


def anywhere():
    return pl.BlockSpec(memory_space=pl.ANY)


def turn(value, shift):
    return pltpu.roll(value.astype(F32), shift, 0).astype(value.dtype)


def convolve(rows, taps):
    out = []
    for r in range(len(rows) - 2):
        part = [
            taps[e] * rows[r] + taps[3 + e] * rows[r + 1] + taps[6 + e] * rows[r + 2]
            for e in range(3)
        ]
        first = turn(part[0][COLS - 1], 1)
        last = turn(part[2][0], SUBL - 1)
        west = jnp.concatenate([first[None], part[0][:-1]], axis=0)
        east = jnp.concatenate([part[2][1:], last[None]], axis=0)
        out.append(part[1] + west + east)
    return out


def fill_taps(tap_ref, kernel_ref, b, flip):
    for a in range(3):
        for e in range(3):
            row = kernel_ref[b, a, e : e + 1, :]
            at = (2 - a) * 3 + 2 - e if flip else a * 3 + e
            tap_ref[at] = jnp.broadcast_to(row, (SUBL, HID)).astype(BF)


def taps_of(tap_ref):
    return [tap_ref[t] for t in range(9)]


def flat(rows):
    return jnp.concatenate([row.reshape(WIDE, HID) for row in rows], axis=0)


def twice(value):
    return jnp.concatenate([value, value], axis=1)


def gelu_pair(pre):
    v = pre.astype(BF)
    u = v * v
    t = jnp.tanh(v * (u * CUBIC + SQRT_TWO_PI))
    w = 1.0 + t
    return v * w, w * (1.0 + (v * (u * (3.0 * CUBIC) + SQRT_TWO_PI)) * (1.0 - t))


def times_transposed(left, right):
    return lax.dot_general(left, right, (((1,), (1,)), ((), ())), preferred_element_type=F32)


def normalize(spatial, mean_ref):
    square = (spatial * spatial).astype(BF)
    mean = jnp.dot(square, mean_ref[...], preferred_element_type=F32)
    inv = lax.rsqrt(mean + EPSILON)
    return inv, spatial * twice(inv.astype(BF))


def forward(b, hat, gain_ref, up_ref, down_ref, act_ref, slope_ref):
    normed = hat * gain_ref[b : b + 1, :].astype(BF)
    for j in range(EXP // CHUNK):
        cut = slice(j * CHUNK, (j + 1) * CHUNK)
        pre = jnp.dot(normed, up_ref[b, :, cut], preferred_element_type=F32)
        act, slope = gelu_pair(pre)
        act_ref[:, cut] = act
        slope_ref[:, cut] = slope
    return 0.5 * jnp.dot(act_ref[...], down_ref[b], preferred_element_type=F32)


def backward(b, grad_s, hat, inv, gain_ref, up_ref, down_ref, act_ref, slope_ref, mean_ref):
    for j in range(EXP // CHUNK):
        cut = slice(j * CHUNK, (j + 1) * CHUNK)
        grad_g = times_transposed(grad_s, down_ref[b, cut, :])
        act_ref[:, cut] = grad_g.astype(BF) * slope_ref[:, cut]
    weighted = times_transposed(act_ref[...], up_ref[b]) * (0.5 * gain_ref[b : b + 1, :])
    hat = hat.astype(F32)
    product = (weighted * hat).astype(BF)
    projection = jnp.dot(product, mean_ref[...], preferred_element_type=F32)
    return twice(inv) * (weighted - hat * twice(projection))


def row_mask(first):
    row = lax.axis_index("lat") * LAT + first
    ok = jnp.logical_and(row >= 0, row < lax.axis_size("lat") * LAT)
    return jnp.where(ok, 1.0, 0.0).astype(F32)


def store_rows(ref, base, value, first=None):
    for r in range(R):
        part = value[r * WIDE : (r + 1) * WIDE]
        if first is not None:
            part = part * row_mask(first + r)
        ref[base + r] = part.astype(BF).reshape(COLS, SUBL, HID)


def from_natural(ref):
    return jnp.concatenate([ref[pl.ds(t, SUBL, stride=COLS), :] for t in range(COLS)], axis=0)


def forward_kernel(
    left_ref, main_ref, right_ref, kernel_ref, gain_ref, up_ref, down_ref,
    out_ref, tape_hbm, hat_hbm, inv_hbm,
    hidden, natural, taps, mean_ref, act, slope, hats, invs, sem,
):
    fill_taps(taps, kernel_ref, 0, False)
    mean_ref[...] = jnp.full((HID, LANES), 1.0 / HID, BF)

    @pl.loop(0, LAT + 2 * HALO)
    def _(i):
        for half in range(2):
            lanes = slice(half * LANES, (half + 1) * LANES)
            natural[half, 0:SIDE, :] = left_ref[i, :, lanes].astype(F32)
            natural[half, SIDE : SIDE + LON, :] = main_ref[i, :, lanes].astype(F32)
            natural[half, SIDE + LON : WIDE, :] = right_ref[i, :, lanes].astype(F32)
            row = from_natural(natural.at[half]).astype(BF)
            hidden[i, :, :, lanes] = row.reshape(COLS, SUBL, LANES)

    def copies(i, slot):
        at = pl.ds(pl.multiple_of((i - 1) * M, 16), M)
        return [
            pltpu.make_async_copy(slope.at[slot], tape_hbm.at[at], sem.at[slot, 0]),
            pltpu.make_async_copy(hats.at[slot], hat_hbm.at[at], sem.at[slot, 1]),
            pltpu.make_async_copy(invs.at[slot], inv_hbm.at[at], sem.at[slot, 2]),
        ]

    steps = HIGH0 // R

    @pl.loop(0, steps)
    def _(i):
        slot = lax.rem(i, 3)

        @pl.when(i >= 4)
        def _():
            for copy in copies(i - 3, slot):
                copy.wait()

        rows = [hidden[i * R + a] for a in range(R + 2)]
        inv, hat = normalize(flat(convolve(rows, taps_of(taps))), mean_ref)
        hats[slot] = hat
        invs[slot] = inv
        branch = forward(0, hat, gain_ref, up_ref, down_ref, act, slope.at[slot])
        store_rows(out_ref, i * R, flat(rows[1:-1]).astype(F32) + branch, i * R + 1 - HALO)

        @pl.when(jnp.logical_and(i >= 1, i < steps - 1))
        def _():
            for copy in copies(i, slot):
                copy.start()

    for i in range(steps - 3, steps - 1):
        for copy in copies(i, i % 3):
            copy.wait()


def main_kernel(
    levels,
    hidden_ref, left_ref, main_ref, right_ref, kernel_ref, gain_ref, up_ref, down_ref,
    dec_ref, enc_ref, tape_hbm, hat_hbm, inv_hbm,
    out_ref,
    taps, mean_ref, natural, act, slope, adjoint, grad_d1, grad_d0, grad1, tape, hats, invs, gathered,
    sem,
):
    copies = [
        pltpu.make_async_copy(tape_hbm, tape, sem.at[0]),
        pltpu.make_async_copy(hat_hbm, hats, sem.at[1]),
        pltpu.make_async_copy(inv_hbm, invs, sem.at[2]),
    ]
    for copy in copies:
        copy.start()
    mean_ref[...] = jnp.full((HID, LANES), 1.0 / HID, BF)
    fill_taps(taps.at[0], kernel_ref, 1, False)
    fill_taps(taps.at[1], kernel_ref, 1, True)
    fill_taps(taps.at[2], kernel_ref, 0, True)

    @pl.loop(0, HIGH1 // R)
    def _(i):
        rows = [hidden_ref[i * R + a] for a in range(R + 2)]
        inv, hat = normalize(flat(convolve(rows, taps_of(taps.at[0]))), mean_ref)
        branch = forward(1, hat, gain_ref, up_ref, down_ref, act, slope)
        final = (flat(rows[1:-1]).astype(F32) + branch).astype(BF)
        model = jnp.dot(final, dec_ref[...], preferred_element_type=F32)
        fields = []
        for r in range(R):
            pair = []
            for half in range(2):
                lanes = slice(half * LANES, (half + 1) * LANES)
                place = natural.at[2 * r + half]
                place[0:SIDE, :] = left_ref[i * R + r, :, lanes]
                place[SIDE : SIDE + LON, :] = main_ref[i * R + r, :, lanes]
                place[SIDE + LON : WIDE, :] = right_ref[i * R + r, :, lanes]
                pair.append(from_natural(place))
            fields.append((pair[1], pair[0]))
        counts = jnp.concatenate([f[0] for f in fields], axis=0)
        sums = jnp.concatenate([f[1] for f in fields], axis=0)
        adj = (counts[:, :levels] * model - sums[:, :levels]).astype(BF)
        for r in range(R):
            adjoint[i * R + r] = adj[r * WIDE : (r + 1) * WIDE]
        grad_s = times_transposed(adj, dec_ref[...]).astype(BF)
        grad_d = backward(
            1, grad_s, hat, inv, gain_ref, up_ref, down_ref, act, slope, mean_ref
        )
        store_rows(grad_d1, i * R, grad_d)

    for copy in copies:
        copy.wait()

    @pl.loop(0, HIGH2 // R)
    def _(i):
        rows = [grad_d1[i * R + a] for a in range(R + 2)]
        adj = jnp.concatenate([adjoint[i * R + 1 + r] for r in range(R)], axis=0)
        grad = times_transposed(adj, dec_ref[...])
        grad = grad + flat(convolve(rows, taps_of(taps.at[1]))).astype(F32)
        grad_s = grad.astype(BF)
        store_rows(grad1, i * R, grad_s)
        at = pl.ds(pl.multiple_of(i * M, 16), M)
        grad_d = backward(
            0, grad_s, hats[at], invs[at], gain_ref, up_ref, down_ref, act, tape.at[at], mean_ref
        )
        store_rows(grad_d0, i * R, grad_d, i * R - 1)

    @pl.loop(0, LAT // R)
    def _(i):
        rows = [grad_d0[i * R + a] for a in range(R + 2)]
        conv = convolve(rows, taps_of(taps.at[2]))
        for r in range(R):
            total = conv[r].astype(F32) + grad1[i * R + 1 + r].astype(F32)
            halves = []
            for half in range(2):
                place = natural.at[2 * r + half]
                for t in range(COLS):
                    place[pl.ds(t, SUBL, stride=COLS), :] = total[
                        t, :, half * LANES : (half + 1) * LANES
                    ]
                halves.append(place[SIDE : SIDE + LON, :].astype(BF))
            result = times_transposed(enc_ref[...], jnp.concatenate(halves, axis=1))
            for half in range(2):
                gathered[half, pl.ds(i * R + r, enc_ref.shape[0], stride=LAT), :] = result[
                    :, half * LANES : (half + 1) * LANES
                ]

    for half in range(2):
        out_ref[:, half * LANES : (half + 1) * LANES] = gathered[half]


def place_observations(levels, table_ref, out_ref, hot_ref, row_ref, value_ref):
    @pl.when(pl.program_id(0) == 0)
    def _():
        table = table_ref[...]
        flipped = jnp.transpose(table.astype(F32))
        slots = flipped.shape[1]
        column = flipped[levels + 1 : levels + 2, :]
        iota = lax.broadcasted_iota(jnp.int32, (LON, slots), 0).astype(F32)
        hot_ref[...] = jnp.where(iota == column, 1.0, 0.0).astype(BF)
        row_ref[...] = jnp.broadcast_to(flipped[levels : levels + 1, :], (16, slots))
        depth = table[:, levels + 2 : levels + 3].astype(F32)
        lane = lax.broadcasted_iota(jnp.int32, table.shape, 1)
        mask = jnp.where(lane.astype(F32) < depth, 1.0, 0.0)
        value_ref[:, :LANES] = (table.astype(F32) * mask).astype(BF)
        value_ref[:, LANES:] = mask.astype(BF)

    here = pl.program_id(0).astype(F32)
    keep = jnp.where(row_ref[0:1, :] == here, 1.0, 0.0).astype(BF)
    out_ref[0] = jnp.dot(hot_ref[...] * keep, value_ref[...], preferred_element_type=F32)


def pair_shift(low, high, axis, wrap):
    peers = lax.axis_size(axis)
    up = [(i, (i + 1) % peers) for i in range(peers if wrap else peers - 1)]
    down = [(j, i) for i, j in up]
    return lax.ppermute(high, axis, up), lax.ppermute(low, axis, down)


def kernel_params(limit):
    return pltpu.CompilerParams(vmem_limit_bytes=limit * 1024 * 1024)


def params():
    return pltpu.CompilerParams(
        dimension_semantics=("arbitrary",), vmem_limit_bytes=32 * 1024 * 1024
    )


def whole(shape):
    return pl.BlockSpec(shape, lambda *_: (0,) * len(shape))


def body(
    state, enc_weight, kernels, gains, up_weight, down_weight, dec_weight,
    obs_values, obs_cells, obs_depth,
):
    channels = state.shape[0]
    levels = dec_weight.shape[1]
    owners, slots = obs_cells.shape[1:]

    cells = obs_cells[0]
    tags = jnp.stack([cells // LON, cells % LON, obs_depth[0]], axis=-1).astype(BF)
    packed = jnp.concatenate([obs_values[0].astype(BF), tags], axis=-1)
    packed = jnp.pad(packed, ((0, 0), (0, 16 - slots), (0, LANES - levels - 3)))
    table = lax.all_to_all(packed, ("lat", "lon"), split_axis=0, concat_axis=0, tiled=True)

    top, bottom = pair_shift(state[:, :HALO], state[:, LAT - HALO :], "lat", False)
    tall = jnp.concatenate([top, state, bottom], axis=1)
    main = lax.dot_general(
        tall, enc_weight, (((0,), (0,)), ((), ())), preferred_element_type=F32
    ).astype(BF)
    left, right = pair_shift(main[:, :SIDE], main[:, LON - SIDE :], "lon", True)

    mlp = 2 * WIDE * HID * EXP * 2
    hidden, tape, hat, inv = pl.pallas_call(
        forward_kernel,
        out_shape=[
            sds((HIGH0, COLS, SUBL, HID), BF),
            sds((TAPE, EXP), BF),
            sds((TAPE, HID), BF),
            sds((TAPE, LANES), F32),
        ],
        in_specs=[vmem()] * 7,
        out_specs=[vmem()] + [anywhere()] * 3,
        scratch_shapes=[
            pltpu.VMEM((LAT + 2 * HALO, COLS, SUBL, HID), BF),
            pltpu.VMEM((2, WIDE, LANES), F32),
            pltpu.VMEM((9, SUBL, HID), BF),
            pltpu.VMEM((HID, LANES), BF),
            pltpu.VMEM((M, EXP), BF),
            pltpu.VMEM((3, M, EXP), BF),
            pltpu.VMEM((3, M, HID), BF),
            pltpu.VMEM((3, M, LANES), F32),
            pltpu.SemaphoreType.DMA((3, 3)),
        ],
        compiler_params=kernel_params(40),
        cost_estimate=pl.CostEstimate(
            flops=mlp * HIGH0, bytes_accessed=TAPE * EXP * 2, transcendentals=0
        ),
        name="forward_zero",
    )(left, main, right, kernels, gains, up_weight, down_weight)

    table = table.reshape(owners * 16, LANES)
    field = pl.pallas_call(
        functools.partial(place_observations, levels),
        out_shape=sds((LAT, LON, 2 * LANES), F32),
        grid=(LAT,),
        in_specs=[whole(table.shape)],
        out_specs=pl.BlockSpec((1, LON, 2 * LANES), lambda s: (s, 0, 0)),
        scratch_shapes=[
            pltpu.VMEM((LON, owners * 16), BF),
            pltpu.VMEM((16, owners * 16), F32),
            pltpu.VMEM((owners * 16, 2 * LANES), BF),
        ],
        compiler_params=params(),
        cost_estimate=pl.CostEstimate(
            flops=2 * LAT * LON * owners * 16 * 256, bytes_accessed=2**22, transcendentals=0
        ),
        name="place_observations",
    )(table)
    f_top, f_bottom = pair_shift(field[:2], field[LAT - 2 :], "lat", False)
    field = jnp.concatenate([f_top, field, f_bottom], axis=0)
    f_left, f_right = pair_shift(field[:, :SIDE], field[:, LON - SIDE :], "lon", True)

    gradient = pl.pallas_call(
        functools.partial(main_kernel, levels),
        out_shape=sds((channels * LAT, LON), F32),
        in_specs=[vmem()] * 10 + [anywhere()] * 3,
        out_specs=vmem(),
        scratch_shapes=[
            pltpu.VMEM((3, 9, SUBL, HID), BF),
            pltpu.VMEM((HID, LANES), BF),
            pltpu.VMEM((2 * R, WIDE, LANES), F32),
            pltpu.VMEM((M, EXP), BF),
            pltpu.VMEM((M, EXP), BF),
            pltpu.VMEM((HIGH1, WIDE, levels), BF),
            pltpu.VMEM((HIGH1, COLS, SUBL, HID), BF),
            pltpu.VMEM((HIGH2, COLS, SUBL, HID), BF),
            pltpu.VMEM((HIGH2, COLS, SUBL, HID), BF),
            pltpu.VMEM((TAPE, EXP), BF),
            pltpu.VMEM((TAPE, HID), BF),
            pltpu.VMEM((TAPE, LANES), F32),
            pltpu.VMEM((2, channels * LAT, LANES), F32),
            pltpu.SemaphoreType.DMA((3,)),
        ],
        compiler_params=kernel_params(52),
        cost_estimate=pl.CostEstimate(
            flops=mlp * (2 * HIGH1 + HIGH2), bytes_accessed=TAPE * EXP * 2, transcendentals=0
        ),
        name="forward_one_and_adjoint",
    )(
        hidden, f_left, field, f_right, kernels, gains, up_weight, down_weight, dec_weight,
        enc_weight, tape, hat, inv,
    )
    return gradient.reshape(channels, LAT, LON)


def solution(mesh):
    in_specs = (
        P(None, "lat", "lon"),
        P(),
        P(),
        P(),
        P(),
        P(),
        P(),
        P(("lat", "lon"), None, None, None),
        P(("lat", "lon"), None, None),
        P(("lat", "lon"), None, None),
    )
    out_specs = P(None, "lat", "lon")
    return jax.shard_map(body, mesh=mesh, in_specs=in_specs, out_specs=out_specs, check_vma=False)
```

```python
import functools
import math

import jax
import jax.numpy as jnp
from jax import lax
from jax.experimental import pallas as pl
from jax.experimental.pallas import tpu as pltpu
from jax.sharding import PartitionSpec as P

EPSILON = 1e-06
SQRT_TWO_PI = math.sqrt(2.0 / math.pi)
CUBIC = SQRT_TWO_PI * 0.044715
BF = jnp.bfloat16
F32 = jnp.float32

LAT = 16
LON = 256
HID = 256
EXP = 1024
LANES = 128
SIDE = 8
WIDE = LON + 2 * SIDE
SUBL = 16
COLS = WIDE // SUBL
HALO = 4
R = 2
M = R * WIDE
CHUNK = 256
HIGH0 = LAT + 2 * HALO - 2
HIGH1 = HIGH0 - 2
HIGH2 = HIGH1 - 2
TAPE = HIGH2 * WIDE


def sds(shape, dtype):
    return jax.ShapeDtypeStruct(shape, dtype)


def vmem():
    return pl.BlockSpec(memory_space=pltpu.VMEM)


def anywhere():
    return pl.BlockSpec(memory_space=pl.ANY)


def turn(value, shift):
    return pltpu.roll(value.astype(F32), shift, 0).astype(value.dtype)


def convolve(rows, taps):
    out = []
    for r in range(len(rows) - 2):
        part = [
            taps[e] * rows[r] + taps[3 + e] * rows[r + 1] + taps[6 + e] * rows[r + 2]
            for e in range(3)
        ]
        first = turn(part[0][COLS - 1], 1)
        last = turn(part[2][0], SUBL - 1)
        west = jnp.concatenate([first[None], part[0][:-1]], axis=0)
        east = jnp.concatenate([part[2][1:], last[None]], axis=0)
        out.append(part[1] + west + east)
    return out


def fill_taps(tap_ref, kernel_ref, b, flip):
    for a in range(3):
        for e in range(3):
            row = kernel_ref[b, a, e : e + 1, :]
            at = (2 - a) * 3 + 2 - e if flip else a * 3 + e
            tap_ref[at] = jnp.broadcast_to(row, (SUBL, HID)).astype(BF)


def taps_of(tap_ref):
    return [tap_ref[t] for t in range(9)]


def flat(rows):
    return jnp.concatenate([row.reshape(WIDE, HID) for row in rows], axis=0)


def twice(value):
    return jnp.concatenate([value, value], axis=1)


def gelu_pair(pre):
    v = pre.astype(BF)
    u = v * v
    t = jnp.tanh(v * (u * CUBIC + SQRT_TWO_PI))
    w = 1.0 + t
    return v * w, w * (1.0 + (v * (u * (3.0 * CUBIC) + SQRT_TWO_PI)) * (1.0 - t))


def times_transposed(left, right):
    return lax.dot_general(left, right, (((1,), (1,)), ((), ())), preferred_element_type=F32)


def normalize(spatial, mean_ref):
    square = (spatial * spatial).astype(BF)
    mean = jnp.dot(square, mean_ref[...], preferred_element_type=F32)
    inv = lax.rsqrt(mean + EPSILON)
    return inv, spatial * twice(inv.astype(BF))


def forward(b, hat, gain_ref, up_ref, down_ref, act_ref, slope_ref):
    normed = hat * gain_ref[b : b + 1, :].astype(BF)
    for j in range(EXP // CHUNK):
        cut = slice(j * CHUNK, (j + 1) * CHUNK)
        pre = jnp.dot(normed, up_ref[b, :, cut], preferred_element_type=F32)
        act, slope = gelu_pair(pre)
        act_ref[:, cut] = act
        slope_ref[:, cut] = slope
    return 0.5 * jnp.dot(act_ref[...], down_ref[b], preferred_element_type=F32)


def backward(b, grad_s, hat, inv, gain_ref, up_ref, down_ref, act_ref, slope_ref, mean_ref):
    for j in range(EXP // CHUNK):
        cut = slice(j * CHUNK, (j + 1) * CHUNK)
        grad_g = times_transposed(grad_s, down_ref[b, cut, :])
        act_ref[:, cut] = grad_g.astype(BF) * slope_ref[:, cut]
    weighted = times_transposed(act_ref[...], up_ref[b]) * (0.5 * gain_ref[b : b + 1, :])
    hat = hat.astype(F32)
    product = (weighted * hat).astype(BF)
    projection = jnp.dot(product, mean_ref[...], preferred_element_type=F32)
    return twice(inv) * (weighted - hat * twice(projection))


def row_mask(first):
    row = lax.axis_index("lat") * LAT + first
    ok = jnp.logical_and(row >= 0, row < lax.axis_size("lat") * LAT)
    return jnp.where(ok, 1.0, 0.0).astype(F32)


def store_rows(ref, base, value, first=None):
    for r in range(R):
        part = value[r * WIDE : (r + 1) * WIDE]
        if first is not None:
            part = part * row_mask(first + r)
        ref[base + r] = part.astype(BF).reshape(COLS, SUBL, HID)


def from_natural(ref):
    return jnp.concatenate([ref[pl.ds(t, SUBL, stride=COLS), :] for t in range(COLS)], axis=0)


def forward_kernel(
    first, count,
    left_ref, main_ref, right_ref, kernel_ref, gain_ref, up_ref, down_ref,
    out_ref, tape_hbm, hat_hbm, inv_hbm,
    hidden, natural, taps, mean_ref, act, slope, hats, invs, sem,
):
    fill_taps(taps, kernel_ref, 0, False)
    mean_ref[...] = jnp.full((HID, LANES), 1.0 / HID, BF)

    @pl.loop(0, count + 2)
    def _(i):
        for half in range(2):
            lanes = slice(half * LANES, (half + 1) * LANES)
            natural[half, 0:SIDE, :] = left_ref[first + i, :, lanes].astype(F32)
            natural[half, SIDE : SIDE + LON, :] = main_ref[first + i, :, lanes].astype(F32)
            natural[half, SIDE + LON : WIDE, :] = right_ref[first + i, :, lanes].astype(F32)
            row = from_natural(natural.at[half]).astype(BF)
            hidden[i, :, :, lanes] = row.reshape(COLS, SUBL, LANES)

    steps = count // R
    taped = max(1 - first // R, 0)
    ends = min((HIGH0 - first) // R - 1, steps)

    def copies(i, slot):
        at = pl.ds(pl.multiple_of((i - taped) * M, 16), M)
        return [
            pltpu.make_async_copy(slope.at[slot], tape_hbm.at[at], sem.at[slot, 0]),
            pltpu.make_async_copy(hats.at[slot], hat_hbm.at[at], sem.at[slot, 1]),
            pltpu.make_async_copy(invs.at[slot], inv_hbm.at[at], sem.at[slot, 2]),
        ]

    @pl.loop(0, steps)
    def _(i):
        slot = lax.rem(i, 3)

        @pl.when(i >= taped + 3)
        def _():
            for copy in copies(i - 3, slot):
                copy.wait()

        rows = [hidden[i * R + a] for a in range(R + 2)]
        inv, hat = normalize(flat(convolve(rows, taps_of(taps))), mean_ref)
        hats[slot] = hat
        invs[slot] = inv
        branch = forward(0, hat, gain_ref, up_ref, down_ref, act, slope.at[slot])
        total = flat(rows[1:-1]).astype(F32) + branch
        store_rows(out_ref, i * R, total, first + i * R + 1 - HALO)

        @pl.when(jnp.logical_and(i >= taped, i < ends))
        def _():
            for copy in copies(i, slot):
                copy.start()

    for i in range(max(taped, steps - 3), ends):
        for copy in copies(i, i % 3):
            copy.wait()


def main_kernel(
    levels,
    above_ref, below_ref, left_ref, main_ref, right_ref, kernel_ref, gain_ref, up_ref, down_ref,
    dec_ref, enc_ref, hidden_a, tape_a, hat_a, inv_a, hidden_b, tape_b, hat_b, inv_b,
    out_ref,
    hidden, taps, mean_ref, natural, act, slope, adjoint, grad_d1, grad_d0, grad1,
    tape, hats, invs, gathered, sem,
):
    rows_a = hidden_a.shape[0]
    cells_a = tape_a.shape[0]
    early = [
        pltpu.make_async_copy(hidden_a, hidden.at[:rows_a], sem.at[0]),
        pltpu.make_async_copy(hidden_b, hidden.at[rows_a:], sem.at[1]),
    ]
    copies = [
        pltpu.make_async_copy(tape_a, tape.at[:cells_a], sem.at[2]),
        pltpu.make_async_copy(tape_b, tape.at[cells_a:], sem.at[3]),
        pltpu.make_async_copy(hat_a, hats.at[:cells_a], sem.at[4]),
        pltpu.make_async_copy(hat_b, hats.at[cells_a:], sem.at[5]),
        pltpu.make_async_copy(inv_a, invs.at[:cells_a], sem.at[6]),
        pltpu.make_async_copy(inv_b, invs.at[cells_a:], sem.at[7]),
    ]
    for copy in early + copies:
        copy.start()
    mean_ref[...] = jnp.full((HID, LANES), 1.0 / HID, BF)
    fill_taps(taps.at[0], kernel_ref, 1, False)
    fill_taps(taps.at[1], kernel_ref, 1, True)
    fill_taps(taps.at[2], kernel_ref, 0, True)
    for copy in early:
        copy.wait()
    last = HIGH1 // R - 1

    @pl.loop(0, HIGH1 // R)
    def _(i):
        for edge, ref in ((0, above_ref), (last, below_ref)):

            @pl.when(i == edge)
            def _():
                for r in range(R):
                    for half in range(2):
                        lanes = slice(half * LANES, (half + 1) * LANES)
                        natural[2 * r + half] = ref[r, :, lanes].astype(F32)

        @pl.when(jnp.logical_and(i > 0, i < last))
        def _():
            for r in range(R):
                for half in range(2):
                    lanes = slice(half * LANES, (half + 1) * LANES)
                    place = natural.at[2 * r + half]
                    row = (i - 1) * R + r
                    place[0:SIDE, :] = left_ref[row, :, lanes].astype(F32)
                    place[SIDE : SIDE + LON, :] = main_ref[row, :, lanes]
                    place[SIDE + LON : WIDE, :] = right_ref[row, :, lanes].astype(F32)

        rows = [hidden[i * R + a] for a in range(R + 2)]
        inv, hat = normalize(flat(convolve(rows, taps_of(taps.at[0]))), mean_ref)
        branch = forward(1, hat, gain_ref, up_ref, down_ref, act, slope)
        final = (flat(rows[1:-1]).astype(F32) + branch).astype(BF)
        model = jnp.dot(final, dec_ref[...], preferred_element_type=F32)
        sums = jnp.concatenate([from_natural(natural.at[2 * r]) for r in range(R)], axis=0)
        counts = jnp.concatenate([from_natural(natural.at[2 * r + 1]) for r in range(R)], axis=0)
        adj = (counts[:, :levels] * model - sums[:, :levels]).astype(BF)
        for r in range(R):
            adjoint[i * R + r] = adj[r * WIDE : (r + 1) * WIDE]
        grad_s = times_transposed(adj, dec_ref[...]).astype(BF)
        grad_d = backward(
            1, grad_s, hat, inv, gain_ref, up_ref, down_ref, act, slope, mean_ref
        )
        store_rows(grad_d1, i * R, grad_d)

    for copy in copies:
        copy.wait()

    @pl.loop(0, HIGH2 // R)
    def _(i):
        rows = [grad_d1[i * R + a] for a in range(R + 2)]
        adj = jnp.concatenate([adjoint[i * R + 1 + r] for r in range(R)], axis=0)
        grad = times_transposed(adj, dec_ref[...])
        grad = grad + flat(convolve(rows, taps_of(taps.at[1]))).astype(F32)
        grad_s = grad.astype(BF)
        store_rows(grad1, i * R, grad_s)
        at = pl.ds(pl.multiple_of(i * M, 16), M)
        grad_d = backward(
            0, grad_s, hats[at], invs[at], gain_ref, up_ref, down_ref, act, tape.at[at], mean_ref
        )
        store_rows(grad_d0, i * R, grad_d, i * R - 1)

    @pl.loop(0, LAT // R)
    def _(i):
        rows = [grad_d0[i * R + a] for a in range(R + 2)]
        conv = convolve(rows, taps_of(taps.at[2]))
        for r in range(R):
            total = conv[r].astype(F32) + grad1[i * R + 1 + r].astype(F32)
            halves = []
            for half in range(2):
                place = natural.at[2 * r + half]
                for t in range(COLS):
                    place[pl.ds(t, SUBL, stride=COLS), :] = total[
                        t, :, half * LANES : (half + 1) * LANES
                    ]
                halves.append(place[SIDE : SIDE + LON, :].astype(BF))
            result = times_transposed(enc_ref[...], jnp.concatenate(halves, axis=1))
            for half in range(2):
                gathered[half, pl.ds(i * R + r, enc_ref.shape[0], stride=LAT), :] = result[
                    :, half * LANES : (half + 1) * LANES
                ]

    for half in range(2):
        out_ref[:, half * LANES : (half + 1) * LANES] = gathered[half]


def pack_observations(value_ref, cell_ref, depth_ref, out_ref, flipped, spread):
    used = value_ref.shape[0]
    slots = cell_ref.shape[0]
    cells = cell_ref[...]
    row = lax.shift_right_logical(cells, LON.bit_length() - 1)
    flipped[:used] = value_ref[...]
    flipped[used : used + slots] = row.astype(F32)
    flipped[used + slots : used + 2 * slots] = (cells - row * LON).astype(F32)
    flipped[used + 2 * slots : used + 3 * slots] = depth_ref[...].astype(F32)
    flipped[used + 3 * slots :] = jnp.zeros_like(flipped[used + 3 * slots :])
    for k in range(8):
        block = jnp.transpose(flipped[k * LANES : (k + 1) * LANES, :])
        spread[pl.ds(k, LANES, stride=8), :] = block
    out_ref[...] = spread[...].reshape(LANES, 8, LANES).astype(BF)


def place_observations(
    slots, levels, table_ref,
    field_ref, top_ref, bottom_ref, left_ref, right_ref,
    spread, wide, hot, row_ref, values,
):
    spread[...] = table_ref[...].astype(F32).reshape(LANES * 8, LANES)
    for k in range(8):
        wide[:, k * LANES : (k + 1) * LANES] = spread[pl.ds(k, LANES, stride=8), :]
    used = slots * levels
    base = used // LANES * LANES
    tags = jnp.transpose(wide[:, base : base + LANES])
    lane = lax.broadcasted_iota(jnp.int32, (LANES, levels), 1).astype(F32)
    column = lax.broadcasted_iota(jnp.int32, (LON, LANES), 0).astype(F32)
    at = used - base
    values[...] = jnp.zeros_like(values)
    for q in range(slots):
        part = slice(q * LANES, (q + 1) * LANES)
        depth = wide[:, used + 2 * slots + q : used + 2 * slots + q + 1]
        mask = jnp.where(lane < depth, 1.0, 0.0)
        values[part, :levels] = (wide[:, q * levels : (q + 1) * levels] * mask).astype(BF)
        values[part, LANES : LANES + levels] = mask.astype(BF)
        row_ref[0:1, part] = tags[at + q : at + q + 1, :]
        where = tags[at + slots + q : at + slots + q + 1, :]
        hot[:, part] = jnp.where(column == where, 1.0, 0.0).astype(BF)

    group = 4

    @pl.loop(0, LAT // group)
    def _(i):
        here = [
            jnp.where(row_ref[0:1, :] == (i * group + r).astype(F32), 1.0, 0.0).astype(BF)
            for r in range(group)
        ]
        left = jnp.concatenate([hot[...] * keep for keep in here], axis=0)
        total = jnp.dot(left, values[...], preferred_element_type=F32)
        for r in range(group):
            row = total[r * LON : (r + 1) * LON]
            field_ref[i * group + r] = row
            left_ref[i * group + r] = row[:SIDE].astype(BF)
            right_ref[i * group + r] = row[LON - SIDE :].astype(BF)

    for r in range(R):
        top_ref[r] = field_ref[r].astype(BF)
        bottom_ref[r] = field_ref[LAT - R + r].astype(BF)


def pair_shift(low, high, axis, wrap):
    peers = lax.axis_size(axis)
    up = [(i, (i + 1) % peers) for i in range(peers if wrap else peers - 1)]
    down = [(j, i) for i, j in up]
    return lax.ppermute(high, axis, up), lax.ppermute(low, axis, down)


def kernel_params(limit):
    return pltpu.CompilerParams(vmem_limit_bytes=limit * 1024 * 1024)


def body(
    state, enc_weight, kernels, gains, up_weight, down_weight, dec_weight,
    obs_values, obs_cells, obs_depth,
):
    channels = state.shape[0]
    levels = dec_weight.shape[1]
    owners, slots = obs_cells.shape[1:]

    edges = lax.optimization_barrier((state[:, :HALO], state[:, LAT - HALO :], obs_cells))
    top, bottom = pair_shift(edges[0], edges[1], "lat", False)

    packed = pl.pallas_call(
        pack_observations,
        out_shape=sds((owners, 8, LANES), BF),
        in_specs=[vmem()] * 3,
        out_specs=vmem(),
        scratch_shapes=[pltpu.VMEM((8 * LANES, LANES), F32)] * 2,
        compiler_params=kernel_params(16),
        name="pack_observations",
    )(
        obs_values[0].transpose(1, 2, 0).reshape(slots * levels, owners),
        edges[2][0].T,
        obs_depth[0].T,
    )
    table = lax.all_to_all(packed, ("lat", "lon"), split_axis=0, concat_axis=0, tiled=True)

    tall = jnp.concatenate([top, state, bottom], axis=1)
    main = lax.dot_general(
        tall, enc_weight, (((0,), (0,)), ((), ())), preferred_element_type=F32
    ).astype(BF)
    left, right = pair_shift(main[:, :SIDE], main[:, LON - SIDE :], "lon", True)

    mlp = 2 * WIDE * HID * EXP * 2

    def forward_zero(first, count, left, main, right):
        cells = min(count, HIGH0 - R - first, first + count - R) * WIDE
        return pl.pallas_call(
            functools.partial(forward_kernel, first, count),
            out_shape=[
                sds((count, COLS, SUBL, HID), BF),
                sds((cells, EXP), BF),
                sds((cells, HID), BF),
                sds((cells, LANES), F32),
            ],
            in_specs=[vmem()] * 7,
            out_specs=[vmem()] + [anywhere()] * 3,
            scratch_shapes=[
                pltpu.VMEM((count + 2, COLS, SUBL, HID), BF),
                pltpu.VMEM((2, WIDE, LANES), F32),
                pltpu.VMEM((9, SUBL, HID), BF),
                pltpu.VMEM((HID, LANES), BF),
                pltpu.VMEM((M, EXP), BF),
                pltpu.VMEM((3, M, EXP), BF),
                pltpu.VMEM((3, M, HID), BF),
                pltpu.VMEM((3, M, LANES), F32),
                pltpu.SemaphoreType.DMA((3, 3)),
            ],
            compiler_params=kernel_params(24),
            cost_estimate=pl.CostEstimate(
                flops=mlp * count * 3, bytes_accessed=cells * EXP * 2, transcendentals=0
            ),
            name="forward_zero",
        )(left, main, right, kernels, gains, up_weight, down_weight)

    field, f_top, f_bottom, f_left, f_right = pl.pallas_call(
        functools.partial(place_observations, slots, levels),
        out_shape=[
            sds((LAT, LON, 2 * LANES), F32),
            sds((R, LON, 2 * LANES), BF),
            sds((R, LON, 2 * LANES), BF),
            sds((LAT, SIDE, 2 * LANES), BF),
            sds((LAT, SIDE, 2 * LANES), BF),
        ],
        in_specs=[vmem()],
        out_specs=[vmem()] * 5,
        scratch_shapes=[
            pltpu.VMEM((8 * LANES, LANES), F32),
            pltpu.VMEM((LANES, 8 * LANES), F32),
            pltpu.VMEM((LON, slots * LANES), BF),
            pltpu.VMEM((8, slots * LANES), F32),
            pltpu.VMEM((slots * LANES, 2 * LANES), BF),
        ],
        compiler_params=kernel_params(24),
        cost_estimate=pl.CostEstimate(
            flops=2 * LAT * LON * slots * LANES * 256, bytes_accessed=2**22, transcendentals=0
        ),
        name="place_observations",
    )(table)

    west, east = pair_shift(f_left, f_right, "lon", True)
    first_rows = 12
    main, f_left = lax.optimization_barrier((main, f_left))
    part_a = forward_zero(0, first_rows, left, main, right)
    west, east, main, hidden_a = lax.optimization_barrier((west, east, main, part_a[0]))
    part_a = [hidden_a] + list(part_a[1:])
    low = jnp.concatenate([west[:R], f_top, east[:R]], axis=1)
    high = jnp.concatenate([west[LAT - R :], f_bottom, east[LAT - R :]], axis=1)
    above, below = pair_shift(low, high, "lat", False)
    main, low = lax.optimization_barrier((main, low))
    part_b = forward_zero(first_rows, HIGH0 - first_rows, left, main, right)

    gradient = pl.pallas_call(
        functools.partial(main_kernel, levels),
        out_shape=sds((channels * LAT, LON), F32),
        in_specs=[vmem()] * 11 + [anywhere()] * 8,
        out_specs=vmem(),
        scratch_shapes=[
            pltpu.VMEM((HIGH0, COLS, SUBL, HID), BF),
            pltpu.VMEM((3, 9, SUBL, HID), BF),
            pltpu.VMEM((HID, LANES), BF),
            pltpu.VMEM((2 * R, WIDE, LANES), F32),
            pltpu.VMEM((M, EXP), BF),
            pltpu.VMEM((M, EXP), BF),
            pltpu.VMEM((HIGH1, WIDE, levels), BF),
            pltpu.VMEM((HIGH1, COLS, SUBL, HID), BF),
            pltpu.VMEM((HIGH2, COLS, SUBL, HID), BF),
            pltpu.VMEM((HIGH2, COLS, SUBL, HID), BF),
            pltpu.VMEM((TAPE, EXP), BF),
            pltpu.VMEM((TAPE, HID), BF),
            pltpu.VMEM((TAPE, LANES), F32),
            pltpu.VMEM((2, channels * LAT, LANES), F32),
            pltpu.SemaphoreType.DMA((8,)),
        ],
        compiler_params=kernel_params(40),
        cost_estimate=pl.CostEstimate(
            flops=mlp * (2 * HIGH1 + HIGH2), bytes_accessed=TAPE * EXP * 2, transcendentals=0
        ),
        name="forward_one_and_adjoint",
    )(
        above, below, west, field, east, kernels, gains, up_weight, down_weight, dec_weight,
        enc_weight, *part_a, *part_b,
    )
    return gradient.reshape(channels, LAT, LON)


def solution(mesh):
    in_specs = (
        P(None, "lat", "lon"),
        P(),
        P(),
        P(),
        P(),
        P(),
        P(),
        P(("lat", "lon"), None, None, None),
        P(("lat", "lon"), None, None),
        P(("lat", "lon"), None, None),
    )
    out_specs = P(None, "lat", "lon")
    return jax.shard_map(body, mesh=mesh, in_specs=in_specs, out_specs=out_specs, check_vma=False)
```

```python
import functools
import math

import jax
import jax.numpy as jnp
from jax import lax
from jax.experimental import pallas as pl
from jax.experimental.pallas import tpu as pltpu
from jax.sharding import PartitionSpec as P

EPSILON = 1e-06
SQRT_TWO_PI = math.sqrt(2.0 / math.pi)
CUBIC = SQRT_TWO_PI * 0.044715
BF = jnp.bfloat16
F32 = jnp.float32

LAT = 16
LON = 256
HID = 256
EXP = 1024
LANES = 128
SIDE = 8
WIDE = LON + 2 * SIDE
SUBL = 16
COLS = WIDE // SUBL
HALO = 4
CHUNK = 256
HIGH0 = LAT + 2 * HALO - 2
HIGH1 = HIGH0 - 2
HIGH2 = HIGH1 - 2
TAPE = HIGH2 * WIDE
MLP = 2 * WIDE * HID * EXP * 2
RF = 2
RM = 4
RB = 6
RE = 4
EDGE = 2


def sds(shape, dtype):
    return jax.ShapeDtypeStruct(shape, dtype)


def vmem():
    return pl.BlockSpec(memory_space=pltpu.VMEM)


def anywhere():
    return pl.BlockSpec(memory_space=pl.ANY)


def turn(value, shift):
    return pltpu.roll(value.astype(F32), shift, 0).astype(value.dtype)


def convolve(rows, taps):
    out = []
    for r in range(len(rows) - 2):
        part = [
            taps[e] * rows[r] + taps[3 + e] * rows[r + 1] + taps[6 + e] * rows[r + 2]
            for e in range(3)
        ]
        first = turn(part[0][COLS - 1], 1)
        last = turn(part[2][0], SUBL - 1)
        west = jnp.concatenate([first[None], part[0][:-1]], axis=0)
        east = jnp.concatenate([part[2][1:], last[None]], axis=0)
        out.append(part[1] + west + east)
    return out


def fill_taps(tap_ref, kernel_ref, b, flip):
    for a in range(3):
        for e in range(3):
            row = kernel_ref[b, a, e : e + 1, :]
            at = (2 - a) * 3 + 2 - e if flip else a * 3 + e
            tap_ref[at] = jnp.broadcast_to(row, (SUBL, HID)).astype(BF)


def taps_of(tap_ref):
    return [tap_ref[t] for t in range(9)]


def flat(rows):
    return jnp.concatenate([row.reshape(WIDE, HID) for row in rows], axis=0)


def twice(value):
    return jnp.concatenate([value, value], axis=1)


def gelu_pair(pre):
    v = pre.astype(BF)
    u = v * v
    t = jnp.tanh(v * (u * CUBIC + SQRT_TWO_PI))
    w = 1.0 + t
    return v * w, w * (1.0 + (v * (u * (3.0 * CUBIC) + SQRT_TWO_PI)) * (1.0 - t))


def times_transposed(left, right):
    return lax.dot_general(left, right, (((1,), (1,)), ((), ())), preferred_element_type=F32)


def normalize(spatial, mean_ref):
    square = (spatial * spatial).astype(BF)
    mean = jnp.dot(square, mean_ref[...], preferred_element_type=F32)
    inv = lax.rsqrt(mean + EPSILON)
    return inv, spatial * twice(inv.astype(BF))


def forward(b, hat, gain_ref, up_ref, down_ref, act_ref, slope_ref):
    normed = hat * gain_ref[b : b + 1, :].astype(BF)
    for j in range(EXP // CHUNK):
        cut = slice(j * CHUNK, (j + 1) * CHUNK)
        pre = jnp.dot(normed, up_ref[b, :, cut], preferred_element_type=F32)
        act, slope = gelu_pair(pre)
        act_ref[:, cut] = act
        slope_ref[:, cut] = slope
    return 0.5 * jnp.dot(act_ref[...], down_ref[b], preferred_element_type=F32)


def backward(b, grad_s, hat, inv, gain_ref, up_ref, down_ref, act_ref, slope_ref, mean_ref):
    for j in range(EXP // CHUNK):
        cut = slice(j * CHUNK, (j + 1) * CHUNK)
        grad_g = times_transposed(grad_s, down_ref[b, cut, :])
        act_ref[:, cut] = grad_g.astype(BF) * slope_ref[:, cut]
    weighted = times_transposed(act_ref[...], up_ref[b]) * (0.5 * gain_ref[b : b + 1, :])
    hat = hat.astype(F32)
    product = (weighted * hat).astype(BF)
    projection = jnp.dot(product, mean_ref[...], preferred_element_type=F32)
    return twice(inv) * (weighted - hat * twice(projection))


def row_mask(first):
    row = lax.axis_index("lat") * LAT + first
    ok = jnp.logical_and(row >= 0, row < lax.axis_size("lat") * LAT)
    return jnp.where(ok, 1.0, 0.0).astype(F32)


def store_rows(ref, base, value, first=None):
    for r in range(value.shape[0] // WIDE):
        part = value[r * WIDE : (r + 1) * WIDE]
        if first is not None:
            part = part * row_mask(first + r)
        ref[base + r] = part.astype(BF).reshape(COLS, SUBL, HID)


def from_natural(ref):
    return jnp.concatenate([ref[pl.ds(t, SUBL, stride=COLS), :] for t in range(COLS)], axis=0)


def forward_kernel(
    first, count,
    left_ref, main_ref, right_ref, kernel_ref, gain_ref, up_ref, down_ref,
    out_ref, tape_hbm, hat_hbm, inv_hbm,
    hidden, natural, taps, mean_ref, act, slope, hats, invs, sem,
):
    fill_taps(taps, kernel_ref, 0, False)
    mean_ref[...] = jnp.full((HID, LANES), 1.0 / HID, BF)

    @pl.loop(0, count + 2)
    def _(i):
        for half in range(2):
            lanes = slice(half * LANES, (half + 1) * LANES)
            natural[half, 0:SIDE, :] = left_ref[first + i, :, lanes].astype(F32)
            natural[half, SIDE : SIDE + LON, :] = main_ref[first + i, :, lanes].astype(F32)
            natural[half, SIDE + LON : WIDE, :] = right_ref[first + i, :, lanes].astype(F32)
            row = from_natural(natural.at[half]).astype(BF)
            hidden[i, :, :, lanes] = row.reshape(COLS, SUBL, LANES)

    steps = count // RF
    taped = max(1 - first // RF, 0)
    ends = min((HIGH0 - first) // RF - 1, steps)

    def copies(i, slot):
        at = pl.ds(pl.multiple_of((i - taped) * RF * WIDE, 16), RF * WIDE)
        return [
            pltpu.make_async_copy(slope.at[slot], tape_hbm.at[at], sem.at[slot, 0]),
            pltpu.make_async_copy(hats.at[slot], hat_hbm.at[at], sem.at[slot, 1]),
            pltpu.make_async_copy(invs.at[slot], inv_hbm.at[at], sem.at[slot, 2]),
        ]

    @pl.loop(0, steps)
    def _(i):
        slot = lax.rem(i, 3)

        @pl.when(i >= taped + 3)
        def _():
            for copy in copies(i - 3, slot):
                copy.wait()

        rows = [hidden[i * RF + a] for a in range(RF + 2)]
        inv, hat = normalize(flat(convolve(rows, taps_of(taps))), mean_ref)
        hats[slot] = hat
        invs[slot] = inv
        branch = forward(0, hat, gain_ref, up_ref, down_ref, act, slope.at[slot])
        total = flat(rows[1:-1]).astype(F32) + branch
        store_rows(out_ref, i * RF, total, first + i * RF + 1 - HALO)

        @pl.when(jnp.logical_and(i >= taped, i < ends))
        def _():
            for copy in copies(i, slot):
                copy.start()

    for i in range(max(taped, steps - 3), ends):
        for copy in copies(i, i % 3):
            copy.wait()


def main_kernel(
    levels,
    above_ref, below_ref, left_ref, main_ref, right_ref, kernel_ref, gain_ref, up_ref, down_ref,
    dec_ref, enc_ref, hidden_a, tape_a, hat_a, inv_a, hidden_b, tape_b, hat_b, inv_b,
    out_ref,
    hidden, taps, mean_ref, natural, act, slope, adjoint, grad_d1, grad_d0, grad1,
    tape, hats, invs, gathered, sem,
):
    rows_a = hidden_a.shape[0]
    cells_a = tape_a.shape[0]
    early = [
        pltpu.make_async_copy(hidden_a, hidden.at[:rows_a], sem.at[0]),
        pltpu.make_async_copy(hidden_b, hidden.at[rows_a:], sem.at[1]),
    ]
    copies = [
        pltpu.make_async_copy(tape_a, tape.at[:cells_a], sem.at[2]),
        pltpu.make_async_copy(tape_b, tape.at[cells_a:], sem.at[3]),
        pltpu.make_async_copy(hat_a, hats.at[:cells_a], sem.at[4]),
        pltpu.make_async_copy(hat_b, hats.at[cells_a:], sem.at[5]),
        pltpu.make_async_copy(inv_a, invs.at[:cells_a], sem.at[6]),
        pltpu.make_async_copy(inv_b, invs.at[cells_a:], sem.at[7]),
    ]
    for copy in early + copies:
        copy.start()
    mean_ref[...] = jnp.full((HID, LANES), 1.0 / HID, BF)
    fill_taps(taps.at[0], kernel_ref, 1, False)
    fill_taps(taps.at[1], kernel_ref, 1, True)
    fill_taps(taps.at[2], kernel_ref, 0, True)
    for copy in early:
        copy.wait()
    last = HIGH1 // RM - 1

    @pl.loop(0, HIGH1 // RM)
    def _(i):
        for r in range(RM):
            inner = True
            for edge, ref, at in ((0, above_ref, r), (last, below_ref, r - RM + EDGE)):
                if 0 <= at < EDGE:
                    inner = jnp.logical_and(inner, i != edge)

                    @pl.when(i == edge)
                    def _():
                        for half in range(2):
                            lanes = slice(half * LANES, (half + 1) * LANES)
                            row = ref[at, :, lanes].astype(F32)
                            natural[2 * r + half] = row * row_mask(i * RM + r - EDGE)

            @pl.when(inner)
            def _():
                row = i * RM + r - EDGE
                for half in range(2):
                    lanes = slice(half * LANES, (half + 1) * LANES)
                    place = natural.at[2 * r + half]
                    place[0:SIDE, :] = left_ref[row, :, lanes].astype(F32)
                    place[SIDE : SIDE + LON, :] = main_ref[row, :, lanes]
                    place[SIDE + LON : WIDE, :] = right_ref[row, :, lanes].astype(F32)

        rows = [hidden[i * RM + a] for a in range(RM + 2)]
        inv, hat = normalize(flat(convolve(rows, taps_of(taps.at[0]))), mean_ref)
        branch = forward(1, hat, gain_ref, up_ref, down_ref, act.at[: RM * WIDE], slope)
        final = (flat(rows[1:-1]).astype(F32) + branch).astype(BF)
        model = jnp.dot(final, dec_ref[...], preferred_element_type=F32)
        sums = jnp.concatenate([from_natural(natural.at[2 * r]) for r in range(RM)], axis=0)
        counts = jnp.concatenate([from_natural(natural.at[2 * r + 1]) for r in range(RM)], axis=0)
        adj = (counts[:, :levels] * model - sums[:, :levels]).astype(BF)
        for r in range(RM):
            adjoint[i * RM + r] = adj[r * WIDE : (r + 1) * WIDE]
        grad_s = times_transposed(adj, dec_ref[...]).astype(BF)
        grad_d = backward(
            1, grad_s, hat, inv, gain_ref, up_ref, down_ref, act.at[: RM * WIDE], slope, mean_ref
        )
        store_rows(grad_d1, i * RM, grad_d)

    for copy in copies:
        copy.wait()

    @pl.loop(0, HIGH2 // RB)
    def _(i):
        rows = [grad_d1[i * RB + a] for a in range(RB + 2)]
        adj = jnp.concatenate([adjoint[i * RB + 1 + r] for r in range(RB)], axis=0)
        grad = times_transposed(adj, dec_ref[...])
        grad = grad + flat(convolve(rows, taps_of(taps.at[1]))).astype(F32)
        grad_s = grad.astype(BF)
        store_rows(grad1, i * RB, grad_s)
        at = pl.ds(pl.multiple_of(i * RB * WIDE, 16), RB * WIDE)
        grad_d = backward(
            0, grad_s, hats[at], invs[at], gain_ref, up_ref, down_ref, act.at[: RB * WIDE], tape.at[at],
            mean_ref
        )
        store_rows(grad_d0, i * RB, grad_d, i * RB - 1)

    @pl.loop(0, LAT // RE)
    def _(i):
        rows = [grad_d0[i * RE + a] for a in range(RE + 2)]
        conv = convolve(rows, taps_of(taps.at[2]))
        for r in range(RE):
            total = conv[r].astype(F32) + grad1[i * RE + 1 + r].astype(F32)
            halves = []
            for half in range(2):
                place = natural.at[2 * r + half]
                for t in range(COLS):
                    place[pl.ds(t, SUBL, stride=COLS), :] = total[
                        t, :, half * LANES : (half + 1) * LANES
                    ]
                halves.append(place[SIDE : SIDE + LON, :].astype(BF))
            result = times_transposed(enc_ref[...], jnp.concatenate(halves, axis=1))
            for half in range(2):
                gathered[half, pl.ds(i * RE + r, enc_ref.shape[0], stride=LAT), :] = result[
                    :, half * LANES : (half + 1) * LANES
                ]

    for half in range(2):
        out_ref[:, half * LANES : (half + 1) * LANES] = gathered[half]


def pack_observations(value_ref, cell_ref, depth_ref, out_ref, flipped, spread):
    used = value_ref.shape[0]
    slots = cell_ref.shape[0]
    cells = cell_ref[...]
    row = lax.shift_right_logical(cells, LON.bit_length() - 1)
    flipped[:used] = value_ref[...]
    flipped[used : used + slots] = row.astype(F32)
    flipped[used + slots : used + 2 * slots] = (cells - row * LON).astype(F32)
    flipped[used + 2 * slots : used + 3 * slots] = depth_ref[...].astype(F32)
    flipped[used + 3 * slots :] = jnp.zeros_like(flipped[used + 3 * slots :])
    for k in range(8):
        block = jnp.transpose(flipped[k * LANES : (k + 1) * LANES, :])
        spread[pl.ds(k, LANES, stride=8), :] = block
    out_ref[...] = spread[...].reshape(LANES, 8, LANES).astype(BF)


def place_observations(
    slots, levels, table_ref,
    field_ref, top_ref, bottom_ref, left_ref, right_ref,
    spread, wide, hot, row_ref, values,
):
    spread[...] = table_ref[...].astype(F32).reshape(LANES * 8, LANES)
    for k in range(8):
        wide[:, k * LANES : (k + 1) * LANES] = spread[pl.ds(k, LANES, stride=8), :]
    used = slots * levels
    base = used // LANES * LANES
    tags = jnp.transpose(wide[:, base : base + LANES])
    lane = lax.broadcasted_iota(jnp.int32, (LANES, levels), 1).astype(F32)
    column = lax.broadcasted_iota(jnp.int32, (LON, LANES), 0).astype(F32)
    at = used - base
    values[...] = jnp.zeros_like(values)
    for q in range(slots):
        part = slice(q * LANES, (q + 1) * LANES)
        depth = wide[:, used + 2 * slots + q : used + 2 * slots + q + 1]
        mask = jnp.where(lane < depth, 1.0, 0.0)
        values[part, :levels] = (wide[:, q * levels : (q + 1) * levels] * mask).astype(BF)
        values[part, LANES : LANES + levels] = mask.astype(BF)
        row_ref[0:1, part] = tags[at + q : at + q + 1, :]
        where = tags[at + slots + q : at + slots + q + 1, :]
        hot[:, part] = jnp.where(column == where, 1.0, 0.0).astype(BF)

    group = 4

    @pl.loop(0, LAT // group)
    def _(i):
        here = [
            jnp.where(row_ref[0:1, :] == (i * group + r).astype(F32), 1.0, 0.0).astype(BF)
            for r in range(group)
        ]
        left = jnp.concatenate([hot[...] * keep for keep in here], axis=0)
        total = jnp.dot(left, values[...], preferred_element_type=F32)
        for r in range(group):
            row = total[r * LON : (r + 1) * LON]
            field_ref[i * group + r] = row
            left_ref[i * group + r] = row[:SIDE].astype(BF)
            right_ref[i * group + r] = row[LON - SIDE :].astype(BF)

    for r in range(EDGE):
        top_ref[r] = field_ref[r].astype(BF)
        bottom_ref[r] = field_ref[LAT - EDGE + r].astype(BF)


def pair_shift(low, high, axis):
    peers = lax.axis_size(axis)
    up = [(i, (i + 1) % peers) for i in range(peers)]
    down = [(j, i) for i, j in up]
    return lax.ppermute(high, axis, up), lax.ppermute(low, axis, down)


def kernel_params(limit):
    return pltpu.CompilerParams(vmem_limit_bytes=limit * 1024 * 1024)


def forward_call(first, count, *operands):
    cells = min(count, HIGH0 - 2 - first, first + count - 2) * WIDE
    return pl.pallas_call(
        functools.partial(forward_kernel, first, count),
        out_shape=[
            sds((count, COLS, SUBL, HID), BF),
            sds((cells, EXP), BF),
            sds((cells, HID), BF),
            sds((cells, LANES), F32),
        ],
        in_specs=[vmem()] * 7,
        out_specs=[vmem()] + [anywhere()] * 3,
        scratch_shapes=[
            pltpu.VMEM((count + 2, COLS, SUBL, HID), BF),
            pltpu.VMEM((2, WIDE, LANES), F32),
            pltpu.VMEM((9, SUBL, HID), BF),
            pltpu.VMEM((HID, LANES), BF),
            pltpu.VMEM((RF * WIDE, EXP), BF),
            pltpu.VMEM((3, RF * WIDE, EXP), BF),
            pltpu.VMEM((3, RF * WIDE, HID), BF),
            pltpu.VMEM((3, RF * WIDE, LANES), F32),
            pltpu.SemaphoreType.DMA((3, 3)),
        ],
        compiler_params=kernel_params(62),
        cost_estimate=pl.CostEstimate(
            flops=MLP * count * 3, bytes_accessed=cells * EXP * 2, transcendentals=0
        ),
        name="forward_zero",
    )(*operands)


def main_call(channels, levels, *operands):
    return pl.pallas_call(
        functools.partial(main_kernel, levels),
        out_shape=sds((channels * LAT, LON), F32),
        in_specs=[vmem()] * 11 + [anywhere()] * 8,
        out_specs=vmem(),
        scratch_shapes=[
            pltpu.VMEM((HIGH0, COLS, SUBL, HID), BF),
            pltpu.VMEM((3, 9, SUBL, HID), BF),
            pltpu.VMEM((HID, LANES), BF),
            pltpu.VMEM((2 * max(RM, RE), WIDE, LANES), F32),
            pltpu.VMEM((max(RM, RB) * WIDE, EXP), BF),
            pltpu.VMEM((RM * WIDE, EXP), BF),
            pltpu.VMEM((HIGH1, WIDE, levels), BF),
            pltpu.VMEM((HIGH1, COLS, SUBL, HID), BF),
            pltpu.VMEM((HIGH2, COLS, SUBL, HID), BF),
            pltpu.VMEM((HIGH2, COLS, SUBL, HID), BF),
            pltpu.VMEM((TAPE, EXP), BF),
            pltpu.VMEM((TAPE, HID), BF),
            pltpu.VMEM((TAPE, LANES), F32),
            pltpu.VMEM((2, channels * LAT, LANES), F32),
            pltpu.SemaphoreType.DMA((8,)),
        ],
        compiler_params=kernel_params(48),
        cost_estimate=pl.CostEstimate(
            flops=MLP * (2 * HIGH1 + HIGH2), bytes_accessed=TAPE * EXP * 2, transcendentals=0
        ),
        name="forward_one_and_adjoint",
    )(*operands)


def body(
    state, enc_weight, kernels, gains, up_weight, down_weight, dec_weight,
    obs_values, obs_cells, obs_depth,
):
    channels = state.shape[0]
    levels = dec_weight.shape[1]
    owners, slots = obs_cells.shape[1:]

    edges = lax.optimization_barrier((state[:, :HALO], state[:, LAT - HALO :], obs_cells))
    top, bottom = pair_shift(edges[0], edges[1], "lat")

    packed = pl.pallas_call(
        pack_observations,
        out_shape=sds((owners, 8, LANES), BF),
        in_specs=[vmem()] * 3,
        out_specs=vmem(),
        scratch_shapes=[pltpu.VMEM((8 * LANES, LANES), F32)] * 2,
        compiler_params=kernel_params(16),
        name="pack_observations",
    )(
        obs_values[0].transpose(1, 2, 0).reshape(slots * levels, owners),
        edges[2][0].T,
        obs_depth[0].T,
    )
    table = lax.all_to_all(packed, ("lat", "lon"), split_axis=0, concat_axis=0, tiled=True)

    band = lax.axis_index("lat")
    top = jnp.where(band > 0, top, 0)
    bottom = jnp.where(band < lax.axis_size("lat") - 1, bottom, 0)
    tall = jnp.concatenate([top, state, bottom], axis=1)
    main = lax.dot_general(
        tall, enc_weight, (((0,), (0,)), ((), ())), preferred_element_type=F32
    ).astype(BF)
    left, right = pair_shift(main[:, :SIDE], main[:, LON - SIDE :], "lon")

    field, f_top, f_bottom, f_left, f_right = pl.pallas_call(
        functools.partial(place_observations, slots, levels),
        out_shape=[
            sds((LAT, LON, 2 * LANES), F32),
            sds((EDGE, LON, 2 * LANES), BF),
            sds((EDGE, LON, 2 * LANES), BF),
            sds((LAT, SIDE, 2 * LANES), BF),
            sds((LAT, SIDE, 2 * LANES), BF),
        ],
        in_specs=[vmem()],
        out_specs=[vmem()] * 5,
        scratch_shapes=[
            pltpu.VMEM((8 * LANES, LANES), F32),
            pltpu.VMEM((LANES, 8 * LANES), F32),
            pltpu.VMEM((LON, slots * LANES), BF),
            pltpu.VMEM((8, slots * LANES), F32),
            pltpu.VMEM((slots * LANES, 2 * LANES), BF),
        ],
        compiler_params=kernel_params(24),
        cost_estimate=pl.CostEstimate(
            flops=2 * LAT * LON * slots * LANES * 256, bytes_accessed=2**22, transcendentals=0
        ),
        name="place_observations",
    )(table)

    west, east = pair_shift(f_left, f_right, "lon")
    first_rows = 12
    main, f_left = lax.optimization_barrier((main, f_left))
    part_a = forward_call(
        0, first_rows, left, main, right, kernels, gains, up_weight, down_weight
    )
    west, east, main, hidden_a = lax.optimization_barrier((west, east, main, part_a[0]))
    part_a = [hidden_a] + list(part_a[1:])
    low = jnp.concatenate([west[:EDGE], f_top, east[:EDGE]], axis=1)
    high = jnp.concatenate([west[LAT - EDGE :], f_bottom, east[LAT - EDGE :]], axis=1)
    above, below = pair_shift(low, high, "lat")
    main, low = lax.optimization_barrier((main, low))
    part_b = forward_call(
        first_rows, HIGH0 - first_rows, left, main, right, kernels, gains, up_weight, down_weight
    )

    gradient = main_call(
        channels, levels, above, below, west, field, east, kernels, gains, up_weight,
        down_weight, dec_weight, enc_weight, *part_a, *part_b,
    )
    return gradient.reshape(channels, LAT, LON)


def solution(mesh):
    in_specs = (
        P(None, "lat", "lon"),
        P(),
        P(),
        P(),
        P(),
        P(),
        P(),
        P(("lat", "lon"), None, None, None),
        P(("lat", "lon"), None, None),
        P(("lat", "lon"), None, None),
    )
    out_specs = P(None, "lat", "lon")
    return jax.shard_map(body, mesh=mesh, in_specs=in_specs, out_specs=out_specs, check_vma=False)
```

```python
import functools
import math

import jax
import jax.numpy as jnp
from jax import lax
from jax.experimental import pallas as pl
from jax.experimental.pallas import tpu as pltpu
from jax.sharding import PartitionSpec as P

EPSILON = 1e-06
SQRT_TWO_PI = math.sqrt(2.0 / math.pi)
CUBIC = SQRT_TWO_PI * 0.044715
BF = jnp.bfloat16
F32 = jnp.float32

LAT = 16
LON = 256
HID = 256
EXP = 1024
LANES = 128
SIDE = 8
WIDE = LON + 2 * SIDE
SUBL = 16
COLS = WIDE // SUBL
HALO = 4
CHUNK = 256
HIGH0 = LAT + 2 * HALO - 2
HIGH1 = HIGH0 - 2
HIGH2 = HIGH1 - 2
TAPE = HIGH2 * WIDE
MLP = 2 * WIDE * HID * EXP * 2
RF = 2
RM = 4
RB = 6
RE = 4
EDGE = 2


def sds(shape, dtype):
    return jax.ShapeDtypeStruct(shape, dtype)


def vmem():
    return pl.BlockSpec(memory_space=pltpu.VMEM)


def anywhere():
    return pl.BlockSpec(memory_space=pl.ANY)


def turn(value, shift):
    return pltpu.roll(value.astype(F32), shift, 0).astype(value.dtype)


def convolve(rows, taps):
    out = []
    for r in range(len(rows) - 2):
        part = [
            taps[e] * rows[r] + taps[3 + e] * rows[r + 1] + taps[6 + e] * rows[r + 2]
            for e in range(3)
        ]
        first = turn(part[0][COLS - 1], 1)
        last = turn(part[2][0], SUBL - 1)
        west = jnp.concatenate([first[None], part[0][:-1]], axis=0)
        east = jnp.concatenate([part[2][1:], last[None]], axis=0)
        out.append(part[1] + west + east)
    return out


def fill_taps(tap_ref, kernel_ref, b, flip):
    for a in range(3):
        for e in range(3):
            row = kernel_ref[b, a, e : e + 1, :]
            at = (2 - a) * 3 + 2 - e if flip else a * 3 + e
            tap_ref[at] = jnp.broadcast_to(row, (SUBL, HID)).astype(BF)


def taps_of(tap_ref):
    return [tap_ref[t] for t in range(9)]


def flat(rows):
    return jnp.concatenate([row.reshape(WIDE, HID) for row in rows], axis=0)


def twice(value):
    return jnp.concatenate([value, value], axis=1)


def gelu_pair(pre):
    v = pre.astype(BF)
    u = v * v
    t = jnp.tanh(v * (u * CUBIC + SQRT_TWO_PI))
    w = 1.0 + t
    return v * w, w * (1.0 + (v * (u * (3.0 * CUBIC) + SQRT_TWO_PI)) * (1.0 - t))


def times_transposed(left, right):
    return lax.dot_general(left, right, (((1,), (1,)), ((), ())), preferred_element_type=F32)


def normalize(spatial, mean_ref):
    square = (spatial * spatial).astype(BF)
    mean = jnp.dot(square, mean_ref[...], preferred_element_type=F32)
    inv = lax.rsqrt(mean + EPSILON)
    return inv, spatial * twice(inv.astype(BF))


def forward(b, hat, gain_ref, up_ref, down_ref, act_ref, slope_ref):
    normed = hat * gain_ref[b : b + 1, :].astype(BF)
    for j in range(EXP // CHUNK):
        cut = slice(j * CHUNK, (j + 1) * CHUNK)
        pre = jnp.dot(normed, up_ref[b, :, cut], preferred_element_type=F32)
        act, slope = gelu_pair(pre)
        act_ref[:, cut] = act
        slope_ref[:, cut] = slope
    return 0.5 * jnp.dot(act_ref[...], down_ref[b], preferred_element_type=F32)


def backward(b, grad_s, hat, inv, gain_ref, up_ref, down_ref, act_ref, slope_ref, mean_ref):
    for j in range(EXP // CHUNK):
        cut = slice(j * CHUNK, (j + 1) * CHUNK)
        grad_g = times_transposed(grad_s, down_ref[b, cut, :])
        act_ref[:, cut] = grad_g.astype(BF) * slope_ref[:, cut]
    weighted = times_transposed(act_ref[...], up_ref[b]) * (0.5 * gain_ref[b : b + 1, :])
    hat = hat.astype(F32)
    product = (weighted * hat).astype(BF)
    projection = jnp.dot(product, mean_ref[...], preferred_element_type=F32)
    return twice(inv) * (weighted - hat * twice(projection))


def row_mask(first):
    row = lax.axis_index("lat") * LAT + first
    ok = jnp.logical_and(row >= 0, row < lax.axis_size("lat") * LAT)
    return jnp.where(ok, 1.0, 0.0).astype(F32)


def store_rows(ref, base, value, first=None):
    for r in range(value.shape[0] // WIDE):
        part = value[r * WIDE : (r + 1) * WIDE]
        if first is not None:
            part = part * row_mask(first + r)
        ref[base + r] = part.astype(BF).reshape(COLS, SUBL, HID)


def from_natural(ref):
    return jnp.concatenate([ref[pl.ds(t, SUBL, stride=COLS), :] for t in range(COLS)], axis=0)


def forward_kernel(
    first, count,
    left_ref, main_ref, right_ref, kernel_ref, gain_ref, up_ref, down_ref, *rest
):
    (
        out_all, tape_all, hat_all, inv_all,
        hidden, natural, taps, mean_ref, act, slope, hats, invs, outs, sem,
    ) = rest[-14:]
    fill_taps(taps, kernel_ref, 0, False)
    mean_ref[...] = jnp.full((HID, LANES), 1.0 / HID, BF)

    @pl.loop(0, count + 2)
    def _(i):
        for half in range(2):
            lanes = slice(half * LANES, (half + 1) * LANES)
            natural[half, 0:SIDE, :] = left_ref[first + i, :, lanes].astype(F32)
            natural[half, SIDE : SIDE + LON, :] = main_ref[first + i, :, lanes].astype(F32)
            natural[half, SIDE + LON : WIDE, :] = right_ref[first + i, :, lanes].astype(F32)
            row = from_natural(natural.at[half]).astype(BF)
            hidden[i, :, :, lanes] = row.reshape(COLS, SUBL, LANES)

    steps = count // RF
    taped = max(1 - first // RF, 0)
    ends = min((HIGH0 - first) // RF - 1, steps)

    def kept(i, slot):
        at = pl.ds(first + i * RF, RF)
        return [pltpu.make_async_copy(outs.at[slot], out_all.at[at], sem.at[slot, 3])]

    def copies(i, slot):
        at = pl.ds(pl.multiple_of((first // RF + i - 1) * RF * WIDE, 16), RF * WIDE)
        return [
            pltpu.make_async_copy(slope.at[slot], tape_all.at[at], sem.at[slot, 0]),
            pltpu.make_async_copy(hats.at[slot], hat_all.at[at], sem.at[slot, 1]),
            pltpu.make_async_copy(invs.at[slot], inv_all.at[at], sem.at[slot, 2]),
        ]

    @pl.loop(0, steps)
    def _(i):
        slot = lax.rem(i, 3)

        @pl.when(i >= 3)
        def _():
            for copy in kept(i - 3, slot):
                copy.wait()

        @pl.when(i >= taped + 3)
        def _():
            for copy in copies(i - 3, slot):
                copy.wait()

        rows = [hidden[i * RF + a] for a in range(RF + 2)]
        inv, hat = normalize(flat(convolve(rows, taps_of(taps))), mean_ref)
        hats[slot] = hat
        invs[slot] = inv
        branch = forward(0, hat, gain_ref, up_ref, down_ref, act, slope.at[slot])
        total = flat(rows[1:-1]).astype(F32) + branch
        store_rows(outs.at[slot], 0, total, first + i * RF + 1 - HALO)
        for copy in kept(i, slot):
            copy.start()

        @pl.when(jnp.logical_and(i >= taped, i < ends))
        def _():
            for copy in copies(i, slot):
                copy.start()

    for i in range(steps - 3, steps):
        for copy in kept(i, i % 3):
            copy.wait()
    for i in range(max(taped, steps - 3), ends):
        for copy in copies(i, i % 3):
            copy.wait()


def main_kernel(
    levels,
    above_ref, below_ref, left_ref, main_ref, right_ref, kernel_ref, gain_ref, up_ref, down_ref,
    dec_ref, enc_ref, hidden, tape, hats, invs,
    out_ref,
    taps, mean_ref, natural, act, slope, adjoint, grad_d1, grad_d0, grad1, gathered,
):
    mean_ref[...] = jnp.full((HID, LANES), 1.0 / HID, BF)
    fill_taps(taps.at[0], kernel_ref, 1, False)
    fill_taps(taps.at[1], kernel_ref, 1, True)
    fill_taps(taps.at[2], kernel_ref, 0, True)
    last = HIGH1 // RM - 1

    @pl.loop(0, HIGH1 // RM)
    def _(i):
        for r in range(RM):
            inner = True
            for edge, ref, at in ((0, above_ref, r), (last, below_ref, r - RM + EDGE)):
                if 0 <= at < EDGE:
                    inner = jnp.logical_and(inner, i != edge)

                    @pl.when(i == edge)
                    def _():
                        for half in range(2):
                            lanes = slice(half * LANES, (half + 1) * LANES)
                            row = ref[at, :, lanes].astype(F32)
                            natural[2 * r + half] = row * row_mask(i * RM + r - EDGE)

            @pl.when(inner)
            def _():
                row = i * RM + r - EDGE
                for half in range(2):
                    lanes = slice(half * LANES, (half + 1) * LANES)
                    place = natural.at[2 * r + half]
                    place[0:SIDE, :] = left_ref[row, :, lanes].astype(F32)
                    place[SIDE : SIDE + LON, :] = main_ref[row, :, lanes]
                    place[SIDE + LON : WIDE, :] = right_ref[row, :, lanes].astype(F32)

        rows = [hidden[i * RM + a] for a in range(RM + 2)]
        inv, hat = normalize(flat(convolve(rows, taps_of(taps.at[0]))), mean_ref)
        branch = forward(1, hat, gain_ref, up_ref, down_ref, act.at[: RM * WIDE], slope)
        final = (flat(rows[1:-1]).astype(F32) + branch).astype(BF)
        model = jnp.dot(final, dec_ref[...], preferred_element_type=F32)
        sums = jnp.concatenate([from_natural(natural.at[2 * r]) for r in range(RM)], axis=0)
        counts = jnp.concatenate([from_natural(natural.at[2 * r + 1]) for r in range(RM)], axis=0)
        adj = (counts[:, :levels] * model - sums[:, :levels]).astype(BF)
        for r in range(RM):
            adjoint[i * RM + r] = adj[r * WIDE : (r + 1) * WIDE]
        grad_s = times_transposed(adj, dec_ref[...]).astype(BF)
        grad_d = backward(
            1, grad_s, hat, inv, gain_ref, up_ref, down_ref, act.at[: RM * WIDE], slope, mean_ref
        )
        store_rows(grad_d1, i * RM, grad_d)

    @pl.loop(0, HIGH2 // RB)
    def _(i):
        rows = [grad_d1[i * RB + a] for a in range(RB + 2)]
        adj = jnp.concatenate([adjoint[i * RB + 1 + r] for r in range(RB)], axis=0)
        grad = times_transposed(adj, dec_ref[...])
        grad = grad + flat(convolve(rows, taps_of(taps.at[1]))).astype(F32)
        grad_s = grad.astype(BF)
        store_rows(grad1, i * RB, grad_s)
        at = pl.ds(pl.multiple_of(i * RB * WIDE, 16), RB * WIDE)
        grad_d = backward(
            0, grad_s, hats[at], invs[at], gain_ref, up_ref, down_ref, act.at[: RB * WIDE], tape.at[at],
            mean_ref
        )
        store_rows(grad_d0, i * RB, grad_d, i * RB - 1)

    @pl.loop(0, LAT // RE)
    def _(i):
        rows = [grad_d0[i * RE + a] for a in range(RE + 2)]
        conv = convolve(rows, taps_of(taps.at[2]))
        for r in range(RE):
            total = conv[r].astype(F32) + grad1[i * RE + 1 + r].astype(F32)
            halves = []
            for half in range(2):
                place = natural.at[2 * r + half]
                for t in range(COLS):
                    place[pl.ds(t, SUBL, stride=COLS), :] = total[
                        t, :, half * LANES : (half + 1) * LANES
                    ]
                halves.append(place[SIDE : SIDE + LON, :].astype(BF))
            result = times_transposed(enc_ref[...], jnp.concatenate(halves, axis=1))
            for half in range(2):
                gathered[half, pl.ds(i * RE + r, enc_ref.shape[0], stride=LAT), :] = result[
                    :, half * LANES : (half + 1) * LANES
                ]

    for half in range(2):
        out_ref[:, half * LANES : (half + 1) * LANES] = gathered[half]


def pack_observations(value_ref, cell_ref, depth_ref, out_ref, flipped, spread):
    used = value_ref.shape[0]
    slots = cell_ref.shape[0]
    cells = cell_ref[...]
    row = lax.shift_right_logical(cells, LON.bit_length() - 1)
    flipped[:used] = value_ref[...]
    flipped[used : used + slots] = row.astype(F32)
    flipped[used + slots : used + 2 * slots] = (cells - row * LON).astype(F32)
    flipped[used + 2 * slots : used + 3 * slots] = depth_ref[...].astype(F32)
    flipped[used + 3 * slots :] = jnp.zeros_like(flipped[used + 3 * slots :])
    for k in range(8):
        block = jnp.transpose(flipped[k * LANES : (k + 1) * LANES, :])
        spread[pl.ds(k, LANES, stride=8), :] = block
    out_ref[...] = spread[...].reshape(LANES, 8, LANES).astype(BF)


def place_observations(
    slots, levels, table_ref,
    field_ref, top_ref, bottom_ref, left_ref, right_ref,
    spread, wide, hot, row_ref, values,
):
    spread[...] = table_ref[...].astype(F32).reshape(LANES * 8, LANES)
    for k in range(8):
        wide[:, k * LANES : (k + 1) * LANES] = spread[pl.ds(k, LANES, stride=8), :]
    used = slots * levels
    base = used // LANES * LANES
    tags = jnp.transpose(wide[:, base : base + LANES])
    lane = lax.broadcasted_iota(jnp.int32, (LANES, levels), 1).astype(F32)
    column = lax.broadcasted_iota(jnp.int32, (LON, LANES), 0).astype(F32)
    at = used - base
    values[...] = jnp.zeros_like(values)
    for q in range(slots):
        part = slice(q * LANES, (q + 1) * LANES)
        depth = wide[:, used + 2 * slots + q : used + 2 * slots + q + 1]
        mask = jnp.where(lane < depth, 1.0, 0.0)
        values[part, :levels] = (wide[:, q * levels : (q + 1) * levels] * mask).astype(BF)
        values[part, LANES : LANES + levels] = mask.astype(BF)
        row_ref[0:1, part] = tags[at + q : at + q + 1, :]
        where = tags[at + slots + q : at + slots + q + 1, :]
        hot[:, part] = jnp.where(column == where, 1.0, 0.0).astype(BF)

    group = 4

    @pl.loop(0, LAT // group)
    def _(i):
        here = [
            jnp.where(row_ref[0:1, :] == (i * group + r).astype(F32), 1.0, 0.0).astype(BF)
            for r in range(group)
        ]
        left = jnp.concatenate([hot[...] * keep for keep in here], axis=0)
        total = jnp.dot(left, values[...], preferred_element_type=F32)
        for r in range(group):
            row = total[r * LON : (r + 1) * LON]
            field_ref[i * group + r] = row
            left_ref[i * group + r] = row[:SIDE].astype(BF)
            right_ref[i * group + r] = row[LON - SIDE :].astype(BF)

    for r in range(EDGE):
        top_ref[r] = field_ref[r].astype(BF)
        bottom_ref[r] = field_ref[LAT - EDGE + r].astype(BF)


def pair_shift(low, high, axis):
    peers = lax.axis_size(axis)
    up = [(i, (i + 1) % peers) for i in range(peers)]
    down = [(j, i) for i, j in up]
    return lax.ppermute(high, axis, up), lax.ppermute(low, axis, down)


def kernel_params(limit):
    return pltpu.CompilerParams(vmem_limit_bytes=limit * 1024 * 1024)


def forward_call(first, count, *operands):
    whole = len(operands) - 7
    return pl.pallas_call(
        functools.partial(forward_kernel, first, count),
        out_shape=[
            sds((HIGH0, COLS, SUBL, HID), BF),
            sds((TAPE, EXP), BF),
            sds((TAPE, HID), BF),
            sds((TAPE, LANES), F32),
        ],
        in_specs=[vmem()] * 7 + [anywhere()] * whole,
        out_specs=[anywhere()] * 4,
        scratch_shapes=[
            pltpu.VMEM((count + 2, COLS, SUBL, HID), BF),
            pltpu.VMEM((2, WIDE, LANES), F32),
            pltpu.VMEM((9, SUBL, HID), BF),
            pltpu.VMEM((HID, LANES), BF),
            pltpu.VMEM((RF * WIDE, EXP), BF),
            pltpu.VMEM((3, RF * WIDE, EXP), BF),
            pltpu.VMEM((3, RF * WIDE, HID), BF),
            pltpu.VMEM((3, RF * WIDE, LANES), F32),
            pltpu.VMEM((3, RF, COLS, SUBL, HID), BF),
            pltpu.SemaphoreType.DMA((3, 4)),
        ],
        input_output_aliases={7 + k: k for k in range(whole)},
        compiler_params=kernel_params(16),
        cost_estimate=pl.CostEstimate(
            flops=MLP * count * 3, bytes_accessed=TAPE * EXP * 2, transcendentals=0
        ),
        name="forward_zero",
    )(*operands)


def main_call(channels, levels, *operands):
    return pl.pallas_call(
        functools.partial(main_kernel, levels),
        out_shape=sds((channels * LAT, LON), F32),
        in_specs=[vmem()] * 15,
        out_specs=vmem(),
        scratch_shapes=[
            pltpu.VMEM((3, 9, SUBL, HID), BF),
            pltpu.VMEM((HID, LANES), BF),
            pltpu.VMEM((2 * max(RM, RE), WIDE, LANES), F32),
            pltpu.VMEM((max(RM, RB) * WIDE, EXP), BF),
            pltpu.VMEM((RM * WIDE, EXP), BF),
            pltpu.VMEM((HIGH1, WIDE, levels), BF),
            pltpu.VMEM((HIGH1, COLS, SUBL, HID), BF),
            pltpu.VMEM((HIGH2, COLS, SUBL, HID), BF),
            pltpu.VMEM((HIGH2, COLS, SUBL, HID), BF),
            pltpu.VMEM((2, channels * LAT, LANES), F32),
        ],
        compiler_params=kernel_params(24),
        cost_estimate=pl.CostEstimate(
            flops=MLP * (2 * HIGH1 + HIGH2), bytes_accessed=TAPE * EXP * 2, transcendentals=0
        ),
        name="forward_one_and_adjoint",
    )(*operands)


def body(
    state, enc_weight, kernels, gains, up_weight, down_weight, dec_weight,
    obs_values, obs_cells, obs_depth,
):
    channels = state.shape[0]
    levels = dec_weight.shape[1]
    owners, slots = obs_cells.shape[1:]

    edges = lax.optimization_barrier((state[:, :HALO], state[:, LAT - HALO :], obs_cells))
    top, bottom = pair_shift(edges[0], edges[1], "lat")

    packed = pl.pallas_call(
        pack_observations,
        out_shape=sds((owners, 8, LANES), BF),
        in_specs=[vmem()] * 3,
        out_specs=vmem(),
        scratch_shapes=[pltpu.VMEM((8 * LANES, LANES), F32)] * 2,
        compiler_params=kernel_params(16),
        name="pack_observations",
    )(
        obs_values[0].transpose(1, 2, 0).reshape(slots * levels, owners),
        edges[2][0].T,
        obs_depth[0].T,
    )
    table = lax.all_to_all(packed, ("lat", "lon"), split_axis=0, concat_axis=0, tiled=True)

    band = lax.axis_index("lat")
    top = jnp.where(band > 0, top, 0)
    bottom = jnp.where(band < lax.axis_size("lat") - 1, bottom, 0)
    tall = jnp.concatenate([top, state, bottom], axis=1)
    main = lax.dot_general(
        tall, enc_weight, (((0,), (0,)), ((), ())), preferred_element_type=F32
    ).astype(BF)
    left, right = pair_shift(main[:, :SIDE], main[:, LON - SIDE :], "lon")

    field, f_top, f_bottom, f_left, f_right = pl.pallas_call(
        functools.partial(place_observations, slots, levels),
        out_shape=[
            sds((LAT, LON, 2 * LANES), F32),
            sds((EDGE, LON, 2 * LANES), BF),
            sds((EDGE, LON, 2 * LANES), BF),
            sds((LAT, SIDE, 2 * LANES), BF),
            sds((LAT, SIDE, 2 * LANES), BF),
        ],
        in_specs=[vmem()],
        out_specs=[vmem()] * 5,
        scratch_shapes=[
            pltpu.VMEM((8 * LANES, LANES), F32),
            pltpu.VMEM((LANES, 8 * LANES), F32),
            pltpu.VMEM((LON, slots * LANES), BF),
            pltpu.VMEM((8, slots * LANES), F32),
            pltpu.VMEM((slots * LANES, 2 * LANES), BF),
        ],
        compiler_params=kernel_params(24),
        cost_estimate=pl.CostEstimate(
            flops=2 * LAT * LON * slots * LANES * 256, bytes_accessed=2**22, transcendentals=0
        ),
        name="place_observations",
    )(table)

    west, east = pair_shift(f_left, f_right, "lon")
    first_rows = 10
    main, f_left = lax.optimization_barrier((main, f_left))
    part_a = forward_call(
        0, first_rows, left, main, right, kernels, gains, up_weight, down_weight
    )
    west, east, main, *part_a = lax.optimization_barrier((west, east, main, *part_a))
    low = jnp.concatenate([west[:EDGE], f_top, east[:EDGE]], axis=1)
    high = jnp.concatenate([west[LAT - EDGE :], f_bottom, east[LAT - EDGE :]], axis=1)
    above, below = pair_shift(low, high, "lat")
    main, low = lax.optimization_barrier((main, low))
    forward = forward_call(
        first_rows, HIGH0 - first_rows, left, main, right, kernels, gains, up_weight, down_weight,
        *part_a,
    )

    gradient = main_call(
        channels, levels, above, below, west, field, east, kernels, gains, up_weight,
        down_weight, dec_weight, enc_weight, *forward,
    )
    return gradient.reshape(channels, LAT, LON)


def solution(mesh):
    in_specs = (
        P(None, "lat", "lon"),
        P(),
        P(),
        P(),
        P(),
        P(),
        P(),
        P(("lat", "lon"), None, None, None),
        P(("lat", "lon"), None, None),
        P(("lat", "lon"), None, None),
    )
    out_specs = P(None, "lat", "lon")
    return jax.shard_map(body, mesh=mesh, in_specs=in_specs, out_specs=out_specs, check_vma=False)
```

```python
import functools
import math

import jax
import jax.numpy as jnp
from jax import lax
from jax.experimental import pallas as pl
from jax.experimental.pallas import tpu as pltpu
from jax.sharding import PartitionSpec as P

EPSILON = 1e-06
SQRT_TWO_PI = math.sqrt(2.0 / math.pi)
CUBIC = SQRT_TWO_PI * 0.044715
BF = jnp.bfloat16
F32 = jnp.float32

LAT = 16
LON = 256
HID = 256
EXP = 1024
LANES = 128
SIDE = 8
WIDE = LON + 2 * SIDE
SUBL = 16
COLS = WIDE // SUBL
HALO = 4
CHUNK = 256
HIGH0 = LAT + 2 * HALO - 2
HIGH1 = HIGH0 - 2
HIGH2 = HIGH1 - 2
TAPE = HIGH2 * WIDE
MLP = 2 * WIDE * HID * EXP * 2
RF = 2
RM = 4
RB = 6
RE = 4
EDGE = 2


def sds(shape, dtype):
    return jax.ShapeDtypeStruct(shape, dtype)


def vmem():
    return pl.BlockSpec(memory_space=pltpu.VMEM)


def anywhere():
    return pl.BlockSpec(memory_space=pl.ANY)


def turn(value, shift):
    return pltpu.roll(value.astype(F32), shift, 0).astype(value.dtype)


def convolve(rows, taps):
    out = []
    for r in range(len(rows) - 2):
        part = [
            taps[e] * rows[r] + taps[3 + e] * rows[r + 1] + taps[6 + e] * rows[r + 2]
            for e in range(3)
        ]
        first = turn(part[0][COLS - 1], 1)
        last = turn(part[2][0], SUBL - 1)
        west = jnp.concatenate([first[None], part[0][:-1]], axis=0)
        east = jnp.concatenate([part[2][1:], last[None]], axis=0)
        out.append(part[1] + west + east)
    return out


def fill_taps(tap_ref, kernel_ref, b, flip):
    for a in range(3):
        for e in range(3):
            row = kernel_ref[b, a, e : e + 1, :]
            at = (2 - a) * 3 + 2 - e if flip else a * 3 + e
            tap_ref[at] = jnp.broadcast_to(row, (SUBL, HID)).astype(BF)


def taps_of(tap_ref):
    return [tap_ref[t] for t in range(9)]


def flat(rows):
    return jnp.concatenate([row.reshape(WIDE, HID) for row in rows], axis=0)


def twice(value):
    return jnp.concatenate([value, value], axis=1)


def gelu_pair(pre):
    v = pre.astype(BF)
    u = v * v
    t = jnp.tanh(v * (u * CUBIC + SQRT_TWO_PI))
    w = 1.0 + t
    return v * w, w * (1.0 + (v * (u * (3.0 * CUBIC) + SQRT_TWO_PI)) * (1.0 - t))


def times_transposed(left, right):
    return lax.dot_general(left, right, (((1,), (1,)), ((), ())), preferred_element_type=F32)


def normalize(spatial, mean_ref):
    square = (spatial * spatial).astype(BF)
    mean = jnp.dot(square, mean_ref[...], preferred_element_type=F32)
    inv = lax.rsqrt(mean + EPSILON).astype(BF)
    return inv, spatial * twice(inv)


def forward(b, hat, gain_ref, up_ref, down_ref, act_ref, slope_ref):
    normed = hat * gain_ref[b : b + 1, :].astype(BF)
    for j in range(EXP // CHUNK):
        cut = slice(j * CHUNK, (j + 1) * CHUNK)
        pre = jnp.dot(normed, up_ref[b, :, cut], preferred_element_type=F32)
        act, slope = gelu_pair(pre)
        act_ref[:, cut] = act
        slope_ref[:, cut] = slope
    return 0.5 * jnp.dot(act_ref[...], down_ref[b], preferred_element_type=F32)


def backward(b, grad_s, hat, inv, gain_ref, up_ref, down_ref, act_ref, slope_ref, mean_ref):
    for j in range(EXP // CHUNK):
        cut = slice(j * CHUNK, (j + 1) * CHUNK)
        grad_g = times_transposed(grad_s, down_ref[b, cut, :])
        act_ref[:, cut] = grad_g.astype(BF) * slope_ref[:, cut]
    weighted = times_transposed(act_ref[...], up_ref[b]) * (0.5 * gain_ref[b : b + 1, :])
    weighted = weighted.astype(BF)
    projection = jnp.dot(weighted * hat, mean_ref[...], preferred_element_type=F32)
    return twice(inv) * (weighted - hat * twice(projection.astype(BF)))


def row_mask(first):
    row = lax.axis_index("lat") * LAT + first
    ok = jnp.logical_and(row >= 0, row < lax.axis_size("lat") * LAT)
    return jnp.where(ok, 1.0, 0.0).astype(F32)


def store_rows(ref, base, value, first=None):
    for r in range(value.shape[0] // WIDE):
        part = value[r * WIDE : (r + 1) * WIDE]
        if first is not None:
            part = part * row_mask(first + r).astype(part.dtype)
        ref[base + r] = part.astype(BF).reshape(COLS, SUBL, HID)


def from_natural(ref):
    return jnp.concatenate([ref[pl.ds(t, SUBL, stride=COLS), :] for t in range(COLS)], axis=0)


def forward_kernel(
    first, count,
    left_ref, main_ref, right_ref, kernel_ref, gain_ref, up_ref, down_ref, *rest
):
    (
        out_all, tape_all, hat_all, inv_all,
        hidden, natural, taps, mean_ref, act, slope, hats, invs, outs, sem,
    ) = rest[-14:]
    fill_taps(taps, kernel_ref, 0, False)
    mean_ref[...] = jnp.full((HID, LANES), 1.0 / HID, BF)

    @pl.loop(0, count + 2)
    def _(i):
        for half in range(2):
            lanes = slice(half * LANES, (half + 1) * LANES)
            natural[half, 0:SIDE, :] = left_ref[first + i, :, lanes].astype(F32)
            natural[half, SIDE : SIDE + LON, :] = main_ref[first + i, :, lanes].astype(F32)
            natural[half, SIDE + LON : WIDE, :] = right_ref[first + i, :, lanes].astype(F32)
            row = from_natural(natural.at[half]).astype(BF)
            hidden[i, :, :, lanes] = row.reshape(COLS, SUBL, LANES)

    steps = count // RF
    taped = max(1 - first // RF, 0)
    ends = min((HIGH0 - first) // RF - 1, steps)

    def kept(i, slot):
        at = pl.ds(first + i * RF, RF)
        return [pltpu.make_async_copy(outs.at[slot], out_all.at[at], sem.at[slot, 3])]

    def copies(i, slot):
        at = pl.ds(pl.multiple_of((first // RF + i - 1) * RF * WIDE, 16), RF * WIDE)
        return [
            pltpu.make_async_copy(slope.at[slot], tape_all.at[at], sem.at[slot, 0]),
            pltpu.make_async_copy(hats.at[slot], hat_all.at[at], sem.at[slot, 1]),
            pltpu.make_async_copy(invs.at[slot], inv_all.at[at], sem.at[slot, 2]),
        ]

    @pl.loop(0, steps)
    def _(i):
        slot = lax.rem(i, 3)

        @pl.when(i >= 3)
        def _():
            for copy in kept(i - 3, slot):
                copy.wait()

        @pl.when(i >= taped + 3)
        def _():
            for copy in copies(i - 3, slot):
                copy.wait()

        rows = [hidden[i * RF + a] for a in range(RF + 2)]
        inv, hat = normalize(flat(convolve(rows, taps_of(taps))), mean_ref)
        hats[slot] = hat
        invs[slot] = inv
        branch = forward(0, hat, gain_ref, up_ref, down_ref, act, slope.at[slot])
        total = flat(rows[1:-1]).astype(F32) + branch
        store_rows(outs.at[slot], 0, total, first + i * RF + 1 - HALO)
        for copy in kept(i, slot):
            copy.start()

        @pl.when(jnp.logical_and(i >= taped, i < ends))
        def _():
            for copy in copies(i, slot):
                copy.start()

    for i in range(steps - 3, steps):
        for copy in kept(i, i % 3):
            copy.wait()
    for i in range(max(taped, steps - 3), ends):
        for copy in copies(i, i % 3):
            copy.wait()


def main_kernel(
    levels,
    above_ref, below_ref, left_ref, main_ref, right_ref, kernel_ref, gain_ref, up_ref, down_ref,
    dec_ref, enc_ref, hidden, tape, hats, invs,
    out_ref,
    taps, mean_ref, natural, act, slope, adjoint, grad_d1, grad_d0, grad1, gathered,
):
    mean_ref[...] = jnp.full((HID, LANES), 1.0 / HID, BF)
    fill_taps(taps.at[0], kernel_ref, 1, False)
    fill_taps(taps.at[1], kernel_ref, 1, True)
    fill_taps(taps.at[2], kernel_ref, 0, True)
    last = HIGH1 // RM - 1

    @pl.loop(0, HIGH1 // RM)
    def _(i):
        for r in range(RM):
            inner = True
            for edge, ref, at in ((0, above_ref, r), (last, below_ref, r - RM + EDGE)):
                if 0 <= at < EDGE:
                    inner = jnp.logical_and(inner, i != edge)

                    @pl.when(i == edge)
                    def _():
                        for half in range(2):
                            lanes = slice(half * LANES, (half + 1) * LANES)
                            row = ref[at, :, lanes].astype(F32)
                            natural[2 * r + half] = row * row_mask(i * RM + r - EDGE)

            @pl.when(inner)
            def _():
                row = i * RM + r - EDGE
                for half in range(2):
                    lanes = slice(half * LANES, (half + 1) * LANES)
                    place = natural.at[2 * r + half]
                    place[0:SIDE, :] = left_ref[row, :, lanes].astype(F32)
                    place[SIDE : SIDE + LON, :] = main_ref[row, :, lanes]
                    place[SIDE + LON : WIDE, :] = right_ref[row, :, lanes].astype(F32)

        rows = [hidden[i * RM + a] for a in range(RM + 2)]
        inv, hat = normalize(flat(convolve(rows, taps_of(taps.at[0]))), mean_ref)
        branch = forward(1, hat, gain_ref, up_ref, down_ref, act.at[: RM * WIDE], slope)
        final = (flat(rows[1:-1]).astype(F32) + branch).astype(BF)
        model = jnp.dot(final, dec_ref[...], preferred_element_type=F32)
        sums = jnp.concatenate([from_natural(natural.at[2 * r]) for r in range(RM)], axis=0)
        counts = jnp.concatenate([from_natural(natural.at[2 * r + 1]) for r in range(RM)], axis=0)
        adj = (counts[:, :levels] * model - sums[:, :levels]).astype(BF)
        for r in range(RM):
            adjoint[i * RM + r] = adj[r * WIDE : (r + 1) * WIDE]
        grad_s = times_transposed(adj, dec_ref[...]).astype(BF)
        grad_d = backward(
            1, grad_s, hat, inv, gain_ref, up_ref, down_ref, act.at[: RM * WIDE], slope, mean_ref
        )
        store_rows(grad_d1, i * RM, grad_d)

    @pl.loop(0, HIGH2 // RB)
    def _(i):
        rows = [grad_d1[i * RB + a] for a in range(RB + 2)]
        adj = jnp.concatenate([adjoint[i * RB + 1 + r] for r in range(RB)], axis=0)
        grad = times_transposed(adj, dec_ref[...])
        grad = grad + flat(convolve(rows, taps_of(taps.at[1]))).astype(F32)
        grad_s = grad.astype(BF)
        store_rows(grad1, i * RB, grad_s)
        at = pl.ds(pl.multiple_of(i * RB * WIDE, 16), RB * WIDE)
        grad_d = backward(
            0, grad_s, hats[at], invs[at], gain_ref, up_ref, down_ref, act.at[: RB * WIDE], tape.at[at],
            mean_ref
        )
        store_rows(grad_d0, i * RB, grad_d, i * RB - 1)

    @pl.loop(0, LAT // RE)
    def _(i):
        rows = [grad_d0[i * RE + a] for a in range(RE + 2)]
        conv = convolve(rows, taps_of(taps.at[2]))
        for r in range(RE):
            total = conv[r].astype(F32) + grad1[i * RE + 1 + r].astype(F32)
            halves = []
            for half in range(2):
                place = natural.at[2 * r + half]
                for t in range(COLS):
                    place[pl.ds(t, SUBL, stride=COLS), :] = total[
                        t, :, half * LANES : (half + 1) * LANES
                    ]
                halves.append(place[SIDE : SIDE + LON, :].astype(BF))
            result = times_transposed(enc_ref[...], jnp.concatenate(halves, axis=1))
            for half in range(2):
                gathered[half, pl.ds(i * RE + r, enc_ref.shape[0], stride=LAT), :] = result[
                    :, half * LANES : (half + 1) * LANES
                ]

    for half in range(2):
        out_ref[:, half * LANES : (half + 1) * LANES] = gathered[half]


def pack_observations(value_ref, cell_ref, depth_ref, out_ref, flipped, spread):
    used = value_ref.shape[0]
    slots = cell_ref.shape[0]
    cells = cell_ref[...]
    row = lax.shift_right_logical(cells, LON.bit_length() - 1)
    flipped[:used] = value_ref[...]
    flipped[used : used + slots] = row.astype(F32)
    flipped[used + slots : used + 2 * slots] = (cells - row * LON).astype(F32)
    flipped[used + 2 * slots : used + 3 * slots] = depth_ref[...].astype(F32)
    flipped[used + 3 * slots :] = jnp.zeros_like(flipped[used + 3 * slots :])
    for k in range(8):
        block = jnp.transpose(flipped[k * LANES : (k + 1) * LANES, :])
        spread[pl.ds(k, LANES, stride=8), :] = block
    out_ref[...] = spread[...].reshape(LANES, 8, LANES).astype(BF)


def place_observations(
    slots, levels, table_ref,
    field_ref, top_ref, bottom_ref, left_ref, right_ref,
    spread, wide, hot, row_ref, values,
):
    spread[...] = table_ref[...].astype(F32).reshape(LANES * 8, LANES)
    for k in range(8):
        wide[:, k * LANES : (k + 1) * LANES] = spread[pl.ds(k, LANES, stride=8), :]
    used = slots * levels
    base = used // LANES * LANES
    tags = jnp.transpose(wide[:, base : base + LANES])
    lane = lax.broadcasted_iota(jnp.int32, (LANES, levels), 1).astype(F32)
    column = lax.broadcasted_iota(jnp.int32, (LON, LANES), 0).astype(F32)
    at = used - base
    values[...] = jnp.zeros_like(values)
    for q in range(slots):
        part = slice(q * LANES, (q + 1) * LANES)
        depth = wide[:, used + 2 * slots + q : used + 2 * slots + q + 1]
        mask = jnp.where(lane < depth, 1.0, 0.0)
        values[part, :levels] = (wide[:, q * levels : (q + 1) * levels] * mask).astype(BF)
        values[part, LANES : LANES + levels] = mask.astype(BF)
        row_ref[0:1, part] = tags[at + q : at + q + 1, :]
        where = tags[at + slots + q : at + slots + q + 1, :]
        hot[:, part] = jnp.where(column == where, 1.0, 0.0).astype(BF)

    group = 8

    @pl.loop(0, LAT // group)
    def _(i):
        here = [
            jnp.where(row_ref[0:1, :] == (i * group + r).astype(F32), 1.0, 0.0).astype(BF)
            for r in range(group)
        ]
        left = jnp.concatenate([hot[...] * keep for keep in here], axis=0)
        total = jnp.dot(left, values[...], preferred_element_type=F32)
        for r in range(group):
            row = total[r * LON : (r + 1) * LON]
            field_ref[i * group + r] = row
            left_ref[i * group + r] = row[:SIDE].astype(BF)
            right_ref[i * group + r] = row[LON - SIDE :].astype(BF)

    for r in range(EDGE):
        top_ref[r] = field_ref[r].astype(BF)
        bottom_ref[r] = field_ref[LAT - EDGE + r].astype(BF)


def pair_shift(low, high, axis):
    peers = lax.axis_size(axis)
    up = [(i, (i + 1) % peers) for i in range(peers)]
    down = [(j, i) for i, j in up]
    return lax.ppermute(high, axis, up), lax.ppermute(low, axis, down)


def kernel_params(limit):
    return pltpu.CompilerParams(vmem_limit_bytes=limit * 1024 * 1024)


def forward_call(first, count, *operands):
    whole = len(operands) - 7
    return pl.pallas_call(
        functools.partial(forward_kernel, first, count),
        out_shape=[
            sds((HIGH0, COLS, SUBL, HID), BF),
            sds((TAPE, EXP), BF),
            sds((TAPE, HID), BF),
            sds((TAPE, LANES), BF),
        ],
        in_specs=[vmem()] * 7 + [anywhere()] * whole,
        out_specs=[anywhere()] * 4,
        scratch_shapes=[
            pltpu.VMEM((count + 2, COLS, SUBL, HID), BF),
            pltpu.VMEM((2, WIDE, LANES), F32),
            pltpu.VMEM((9, SUBL, HID), BF),
            pltpu.VMEM((HID, LANES), BF),
            pltpu.VMEM((RF * WIDE, EXP), BF),
            pltpu.VMEM((3, RF * WIDE, EXP), BF),
            pltpu.VMEM((3, RF * WIDE, HID), BF),
            pltpu.VMEM((3, RF * WIDE, LANES), BF),
            pltpu.VMEM((3, RF, COLS, SUBL, HID), BF),
            pltpu.SemaphoreType.DMA((3, 4)),
        ],
        input_output_aliases={7 + k: k for k in range(whole)},
        compiler_params=kernel_params(16),
        cost_estimate=pl.CostEstimate(
            flops=MLP * count * 3, bytes_accessed=TAPE * EXP * 2, transcendentals=0
        ),
        name="forward_zero",
    )(*operands)


def main_call(channels, levels, *operands):
    return pl.pallas_call(
        functools.partial(main_kernel, levels),
        out_shape=sds((channels * LAT, LON), F32),
        in_specs=[vmem()] * 15,
        out_specs=vmem(),
        scratch_shapes=[
            pltpu.VMEM((3, 9, SUBL, HID), BF),
            pltpu.VMEM((HID, LANES), BF),
            pltpu.VMEM((2 * max(RM, RE), WIDE, LANES), F32),
            pltpu.VMEM((max(RM, RB) * WIDE, EXP), BF),
            pltpu.VMEM((RM * WIDE, EXP), BF),
            pltpu.VMEM((HIGH1, WIDE, levels), BF),
            pltpu.VMEM((HIGH1, COLS, SUBL, HID), BF),
            pltpu.VMEM((HIGH2, COLS, SUBL, HID), BF),
            pltpu.VMEM((HIGH2, COLS, SUBL, HID), BF),
            pltpu.VMEM((2, channels * LAT, LANES), F32),
        ],
        compiler_params=kernel_params(24),
        cost_estimate=pl.CostEstimate(
            flops=MLP * (2 * HIGH1 + HIGH2), bytes_accessed=TAPE * EXP * 2, transcendentals=0
        ),
        name="forward_one_and_adjoint",
    )(*operands)


def body(
    state, enc_weight, kernels, gains, up_weight, down_weight, dec_weight,
    obs_values, obs_cells, obs_depth,
):
    channels = state.shape[0]
    levels = dec_weight.shape[1]
    owners, slots = obs_cells.shape[1:]

    edges = lax.optimization_barrier((state[:, :HALO], state[:, LAT - HALO :], obs_cells))
    top, bottom = pair_shift(edges[0], edges[1], "lat")

    packed = pl.pallas_call(
        pack_observations,
        out_shape=sds((owners, 8, LANES), BF),
        in_specs=[vmem()] * 3,
        out_specs=vmem(),
        scratch_shapes=[pltpu.VMEM((8 * LANES, LANES), F32)] * 2,
        compiler_params=kernel_params(16),
        name="pack_observations",
    )(
        obs_values[0].transpose(1, 2, 0).reshape(slots * levels, owners),
        edges[2][0].T,
        obs_depth[0].T,
    )
    table = lax.all_to_all(packed, ("lat", "lon"), split_axis=0, concat_axis=0, tiled=True)

    band = lax.axis_index("lat")
    top = jnp.where(band > 0, top, 0)
    bottom = jnp.where(band < lax.axis_size("lat") - 1, bottom, 0)
    tall = jnp.concatenate([top, state, bottom], axis=1)
    main = lax.dot_general(
        tall, enc_weight, (((0,), (0,)), ((), ())), preferred_element_type=F32
    ).astype(BF)
    left, right = pair_shift(main[:, :SIDE], main[:, LON - SIDE :], "lon")

    field, f_top, f_bottom, f_left, f_right = pl.pallas_call(
        functools.partial(place_observations, slots, levels),
        out_shape=[
            sds((LAT, LON, 2 * LANES), F32),
            sds((EDGE, LON, 2 * LANES), BF),
            sds((EDGE, LON, 2 * LANES), BF),
            sds((LAT, SIDE, 2 * LANES), BF),
            sds((LAT, SIDE, 2 * LANES), BF),
        ],
        in_specs=[vmem()],
        out_specs=[vmem()] * 5,
        scratch_shapes=[
            pltpu.VMEM((8 * LANES, LANES), F32),
            pltpu.VMEM((LANES, 8 * LANES), F32),
            pltpu.VMEM((LON, slots * LANES), BF),
            pltpu.VMEM((8, slots * LANES), F32),
            pltpu.VMEM((slots * LANES, 2 * LANES), BF),
        ],
        compiler_params=kernel_params(24),
        cost_estimate=pl.CostEstimate(
            flops=2 * LAT * LON * slots * LANES * 256, bytes_accessed=2**22, transcendentals=0
        ),
        name="place_observations",
    )(table)

    west, east = pair_shift(f_left, f_right, "lon")
    first_rows = 10
    main, f_left = lax.optimization_barrier((main, f_left))
    part_a = forward_call(
        0, first_rows, left, main, right, kernels, gains, up_weight, down_weight
    )
    west, east, main, *part_a = lax.optimization_barrier((west, east, main, *part_a))
    low = jnp.concatenate([west[:EDGE], f_top, east[:EDGE]], axis=1)
    high = jnp.concatenate([west[LAT - EDGE :], f_bottom, east[LAT - EDGE :]], axis=1)
    above, below = pair_shift(low, high, "lat")
    main, low = lax.optimization_barrier((main, low))
    forward = forward_call(
        first_rows, HIGH0 - first_rows, left, main, right, kernels, gains, up_weight, down_weight,
        *part_a,
    )

    gradient = main_call(
        channels, levels, above, below, west, field, east, kernels, gains, up_weight,
        down_weight, dec_weight, enc_weight, *forward,
    )
    return gradient.reshape(channels, LAT, LON)


def solution(mesh):
    in_specs = (
        P(None, "lat", "lon"),
        P(),
        P(),
        P(),
        P(),
        P(),
        P(),
        P(("lat", "lon"), None, None, None),
        P(("lat", "lon"), None, None),
        P(("lat", "lon"), None, None),
    )
    out_specs = P(None, "lat", "lon")
    return jax.shard_map(body, mesh=mesh, in_specs=in_specs, out_specs=out_specs, check_vma=False)
```

```python
import functools
import math

import jax
import jax.numpy as jnp
from jax import lax
from jax.experimental import pallas as pl
from jax.experimental.pallas import tpu as pltpu
from jax.sharding import PartitionSpec as P

EPSILON = 1e-06
SQRT_TWO_PI = math.sqrt(2.0 / math.pi)
CUBIC = SQRT_TWO_PI * 0.044715
BF = jnp.bfloat16
F32 = jnp.float32

LAT = 16
LON = 256
HID = 256
EXP = 1024
LANES = 128
SIDE = 8
WIDE = LON + 2 * SIDE
SUBL = 16
COLS = WIDE // SUBL
HALO = 4
CHUNK = 256
HIGH0 = LAT + 2 * HALO - 2
HIGH1 = HIGH0 - 2
HIGH2 = HIGH1 - 2
TAPE = HIGH2 * WIDE
MLP = 2 * WIDE * HID * EXP * 2
RF = 2
RM = 4
RB = 6
RE = 4
EDGE = 2


def sds(shape, dtype):
    return jax.ShapeDtypeStruct(shape, dtype)


def vmem():
    return pl.BlockSpec(memory_space=pltpu.VMEM)


def anywhere():
    return pl.BlockSpec(memory_space=pl.ANY)


def turn(value, shift):
    return pltpu.roll(value.astype(F32), shift, 0).astype(value.dtype)


def convolve(rows, taps):
    out = []
    for r in range(len(rows) - 2):
        part = [
            taps[e] * rows[r] + taps[3 + e] * rows[r + 1] + taps[6 + e] * rows[r + 2]
            for e in range(3)
        ]
        first = turn(part[0][COLS - 1], 1)
        last = turn(part[2][0], SUBL - 1)
        west = jnp.concatenate([first[None], part[0][:-1]], axis=0)
        east = jnp.concatenate([part[2][1:], last[None]], axis=0)
        out.append(part[1] + west + east)
    return out


def fill_taps(tap_ref, kernel_ref, b, flip):
    for a in range(3):
        for e in range(3):
            row = kernel_ref[b, a, e : e + 1, :]
            at = (2 - a) * 3 + 2 - e if flip else a * 3 + e
            tap_ref[at] = jnp.broadcast_to(row, (SUBL, HID)).astype(BF)


def taps_of(tap_ref):
    return [tap_ref[t] for t in range(9)]


def flat(rows):
    return jnp.concatenate([row.reshape(WIDE, HID) for row in rows], axis=0)


def twice(value):
    return jnp.concatenate([value, value], axis=1)


def gelu_pair(pre):
    v = pre.astype(BF)
    u = v * v
    t = jnp.tanh(v * (u * CUBIC + SQRT_TWO_PI))
    w = 1.0 + t
    return v * w, w * (1.0 + (v * (u * (3.0 * CUBIC) + SQRT_TWO_PI)) * (1.0 - t))


def times_transposed(left, right):
    return lax.dot_general(left, right, (((1,), (1,)), ((), ())), preferred_element_type=F32)


def normalize(spatial, mean_ref):
    square = (spatial * spatial).astype(BF)
    mean = jnp.dot(square, mean_ref[...], preferred_element_type=F32)
    inv = lax.rsqrt(mean + EPSILON)
    return inv, spatial * twice(inv.astype(BF))


def forward(b, hat, gain_ref, up_ref, down_ref, act_ref, slope_ref):
    normed = hat * gain_ref[b : b + 1, :].astype(BF)
    for j in range(EXP // CHUNK):
        cut = slice(j * CHUNK, (j + 1) * CHUNK)
        pre = jnp.dot(normed, up_ref[b, :, cut], preferred_element_type=F32)
        act, slope = gelu_pair(pre)
        act_ref[:, cut] = act
        slope_ref[:, cut] = slope
    return 0.5 * jnp.dot(act_ref[...], down_ref[b], preferred_element_type=F32)


def backward(b, grad_s, hat, inv, gain_ref, up_ref, down_ref, act_ref, slope_ref, mean_ref):
    for j in range(EXP // CHUNK):
        cut = slice(j * CHUNK, (j + 1) * CHUNK)
        grad_g = times_transposed(grad_s, down_ref[b, cut, :])
        act_ref[:, cut] = grad_g.astype(BF) * slope_ref[:, cut]
    weighted = times_transposed(act_ref[...], up_ref[b]) * (0.5 * gain_ref[b : b + 1, :])
    weighted = weighted.astype(BF)
    projection = jnp.dot(weighted * hat, mean_ref[...], preferred_element_type=F32)
    return twice(inv.astype(BF)) * (weighted - hat * twice(projection.astype(BF)))


def row_mask(first):
    row = lax.axis_index("lat") * LAT + first
    ok = jnp.logical_and(row >= 0, row < lax.axis_size("lat") * LAT)
    return jnp.where(ok, 1.0, 0.0).astype(F32)


def store_rows(ref, base, value, first=None):
    for r in range(value.shape[0] // WIDE):
        part = value[r * WIDE : (r + 1) * WIDE]
        if first is not None:
            part = part * row_mask(first + r).astype(part.dtype)
        ref[base + r] = part.astype(BF).reshape(COLS, SUBL, HID)


def from_natural(ref):
    return jnp.concatenate([ref[pl.ds(t, SUBL, stride=COLS), :] for t in range(COLS)], axis=0)


def forward_kernel(
    first, count,
    left_ref, main_ref, right_ref, kernel_ref, gain_ref, up_ref, down_ref, *rest
):
    (
        out_all, tape_all, hat_all, inv_all,
        hidden, natural, taps, mean_ref, act, slope, hats, invs, outs, sem,
    ) = rest[-14:]
    fill_taps(taps, kernel_ref, 0, False)
    mean_ref[...] = jnp.full((HID, LANES), 1.0 / HID, BF)

    @pl.loop(0, count + 2)
    def _(i):
        for half in range(2):
            lanes = slice(half * LANES, (half + 1) * LANES)
            natural[half, 0:SIDE, :] = left_ref[first + i, :, lanes].astype(F32)
            natural[half, SIDE : SIDE + LON, :] = main_ref[first + i, :, lanes].astype(F32)
            natural[half, SIDE + LON : WIDE, :] = right_ref[first + i, :, lanes].astype(F32)
            row = from_natural(natural.at[half]).astype(BF)
            hidden[i, :, :, lanes] = row.reshape(COLS, SUBL, LANES)

    steps = count // RF
    taped = max(1 - first // RF, 0)
    ends = min((HIGH0 - first) // RF - 1, steps)

    def kept(i, slot):
        at = pl.ds(first + i * RF, RF)
        return [pltpu.make_async_copy(outs.at[slot], out_all.at[at], sem.at[slot, 3])]

    def copies(i, slot):
        at = pl.ds(pl.multiple_of((first // RF + i - 1) * RF * WIDE, 16), RF * WIDE)
        return [
            pltpu.make_async_copy(slope.at[slot], tape_all.at[at], sem.at[slot, 0]),
            pltpu.make_async_copy(hats.at[slot], hat_all.at[at], sem.at[slot, 1]),
            pltpu.make_async_copy(invs.at[slot], inv_all.at[at], sem.at[slot, 2]),
        ]

    @pl.loop(0, steps)
    def _(i):
        slot = lax.rem(i, 3)

        @pl.when(i >= 3)
        def _():
            for copy in kept(i - 3, slot):
                copy.wait()

        @pl.when(i >= taped + 3)
        def _():
            for copy in copies(i - 3, slot):
                copy.wait()

        rows = [hidden[i * RF + a] for a in range(RF + 2)]
        inv, hat = normalize(flat(convolve(rows, taps_of(taps))), mean_ref)
        hats[slot] = hat
        invs[slot] = inv
        branch = forward(0, hat, gain_ref, up_ref, down_ref, act, slope.at[slot])
        total = flat(rows[1:-1]).astype(F32) + branch
        store_rows(outs.at[slot], 0, total, first + i * RF + 1 - HALO)
        for copy in kept(i, slot):
            copy.start()

        @pl.when(jnp.logical_and(i >= taped, i < ends))
        def _():
            for copy in copies(i, slot):
                copy.start()

    for i in range(steps - 3, steps):
        for copy in kept(i, i % 3):
            copy.wait()
    for i in range(max(taped, steps - 3), ends):
        for copy in copies(i, i % 3):
            copy.wait()


def main_kernel(
    levels,
    above_ref, below_ref, left_ref, main_ref, right_ref, kernel_ref, gain_ref, up_ref, down_ref,
    dec_ref, enc_ref, hidden, tape, hats, invs,
    out_ref,
    taps, mean_ref, natural, act, slope, adjoint, grad_d1, grad_d0, grad1, gathered,
):
    mean_ref[...] = jnp.full((HID, LANES), 1.0 / HID, BF)
    fill_taps(taps.at[0], kernel_ref, 1, False)
    fill_taps(taps.at[1], kernel_ref, 1, True)
    fill_taps(taps.at[2], kernel_ref, 0, True)
    last = HIGH1 // RM - 1

    @pl.loop(0, HIGH1 // RM)
    def _(i):
        for r in range(RM):
            inner = True
            for edge, ref, at in ((0, above_ref, r), (last, below_ref, r - RM + EDGE)):
                if 0 <= at < EDGE:
                    inner = jnp.logical_and(inner, i != edge)

                    @pl.when(i == edge)
                    def _():
                        for half in range(2):
                            lanes = slice(half * LANES, (half + 1) * LANES)
                            row = ref[at, :, lanes].astype(F32)
                            natural[2 * r + half] = row * row_mask(i * RM + r - EDGE)

            @pl.when(inner)
            def _():
                row = i * RM + r - EDGE
                for half in range(2):
                    lanes = slice(half * LANES, (half + 1) * LANES)
                    place = natural.at[2 * r + half]
                    place[0:SIDE, :] = left_ref[row, :, lanes].astype(F32)
                    place[SIDE : SIDE + LON, :] = main_ref[row, :, lanes]
                    place[SIDE + LON : WIDE, :] = right_ref[row, :, lanes].astype(F32)

        rows = [hidden[i * RM + a] for a in range(RM + 2)]
        inv, hat = normalize(flat(convolve(rows, taps_of(taps.at[0]))), mean_ref)
        branch = forward(1, hat, gain_ref, up_ref, down_ref, act.at[: RM * WIDE], slope)
        final = (flat(rows[1:-1]).astype(F32) + branch).astype(BF)
        model = jnp.dot(final, dec_ref[...], preferred_element_type=F32)
        sums = jnp.concatenate([from_natural(natural.at[2 * r]) for r in range(RM)], axis=0)
        counts = jnp.concatenate([from_natural(natural.at[2 * r + 1]) for r in range(RM)], axis=0)
        adj = (counts[:, :levels] * model - sums[:, :levels]).astype(BF)
        for r in range(RM):
            adjoint[i * RM + r] = adj[r * WIDE : (r + 1) * WIDE]
        grad_s = times_transposed(adj, dec_ref[...]).astype(BF)
        grad_d = backward(
            1, grad_s, hat, inv, gain_ref, up_ref, down_ref, act.at[: RM * WIDE], slope, mean_ref
        )
        store_rows(grad_d1, i * RM, grad_d)

    @pl.loop(0, HIGH2 // RB)
    def _(i):
        rows = [grad_d1[i * RB + a] for a in range(RB + 2)]
        adj = jnp.concatenate([adjoint[i * RB + 1 + r] for r in range(RB)], axis=0)
        grad = times_transposed(adj, dec_ref[...])
        grad = grad + flat(convolve(rows, taps_of(taps.at[1]))).astype(F32)
        grad_s = grad.astype(BF)
        store_rows(grad1, i * RB, grad_s)
        at = pl.ds(pl.multiple_of(i * RB * WIDE, 16), RB * WIDE)
        grad_d = backward(
            0, grad_s, hats[at], invs[at], gain_ref, up_ref, down_ref, act.at[: RB * WIDE], tape.at[at],
            mean_ref
        )
        store_rows(grad_d0, i * RB, grad_d, i * RB - 1)

    @pl.loop(0, LAT // RE)
    def _(i):
        rows = [grad_d0[i * RE + a] for a in range(RE + 2)]
        conv = convolve(rows, taps_of(taps.at[2]))
        for r in range(RE):
            total = conv[r].astype(F32) + grad1[i * RE + 1 + r].astype(F32)
            halves = []
            for half in range(2):
                place = natural.at[2 * r + half]
                for t in range(COLS):
                    place[pl.ds(t, SUBL, stride=COLS), :] = total[
                        t, :, half * LANES : (half + 1) * LANES
                    ]
                halves.append(place[SIDE : SIDE + LON, :].astype(BF))
            result = times_transposed(enc_ref[...], jnp.concatenate(halves, axis=1))
            for half in range(2):
                gathered[half, pl.ds(i * RE + r, enc_ref.shape[0], stride=LAT), :] = result[
                    :, half * LANES : (half + 1) * LANES
                ]

    for half in range(2):
        out_ref[:, half * LANES : (half + 1) * LANES] = gathered[half]


def pack_observations(value_ref, cell_ref, depth_ref, out_ref, flipped, spread):
    used = value_ref.shape[0]
    slots = cell_ref.shape[0]
    cells = cell_ref[...]
    row = lax.shift_right_logical(cells, LON.bit_length() - 1)
    flipped[:used] = value_ref[...]
    flipped[used : used + slots] = row.astype(F32)
    flipped[used + slots : used + 2 * slots] = (cells - row * LON).astype(F32)
    flipped[used + 2 * slots : used + 3 * slots] = depth_ref[...].astype(F32)
    flipped[used + 3 * slots :] = jnp.zeros_like(flipped[used + 3 * slots :])
    for k in range(8):
        block = jnp.transpose(flipped[k * LANES : (k + 1) * LANES, :])
        spread[pl.ds(k, LANES, stride=8), :] = block
    out_ref[...] = spread[...].reshape(LANES, 8, LANES).astype(BF)


def place_observations(
    slots, levels, table_ref,
    field_ref, top_ref, bottom_ref, left_ref, right_ref,
    spread, wide, hot, row_ref, values,
):
    spread[...] = table_ref[...].astype(F32).reshape(LANES * 8, LANES)
    for k in range(8):
        wide[:, k * LANES : (k + 1) * LANES] = spread[pl.ds(k, LANES, stride=8), :]
    used = slots * levels
    base = used // LANES * LANES
    tags = jnp.transpose(wide[:, base : base + LANES])
    lane = lax.broadcasted_iota(jnp.int32, (LANES, levels), 1).astype(F32)
    column = lax.broadcasted_iota(jnp.int32, (LON, LANES), 0).astype(F32)
    at = used - base
    values[...] = jnp.zeros_like(values)
    for q in range(slots):
        part = slice(q * LANES, (q + 1) * LANES)
        depth = wide[:, used + 2 * slots + q : used + 2 * slots + q + 1]
        mask = jnp.where(lane < depth, 1.0, 0.0)
        values[part, :levels] = (wide[:, q * levels : (q + 1) * levels] * mask).astype(BF)
        values[part, LANES : LANES + levels] = mask.astype(BF)
        row_ref[0:1, part] = tags[at + q : at + q + 1, :]
        where = tags[at + slots + q : at + slots + q + 1, :]
        hot[:, part] = jnp.where(column == where, 1.0, 0.0).astype(BF)

    group = 8

    @pl.loop(0, LAT // group)
    def _(i):
        here = [
            jnp.where(row_ref[0:1, :] == (i * group + r).astype(F32), 1.0, 0.0).astype(BF)
            for r in range(group)
        ]
        left = jnp.concatenate([hot[...] * keep for keep in here], axis=0)
        total = jnp.dot(left, values[...], preferred_element_type=F32)
        for r in range(group):
            row = total[r * LON : (r + 1) * LON]
            field_ref[i * group + r] = row
            left_ref[i * group + r] = row[:SIDE].astype(BF)
            right_ref[i * group + r] = row[LON - SIDE :].astype(BF)

    for r in range(EDGE):
        top_ref[r] = field_ref[r].astype(BF)
        bottom_ref[r] = field_ref[LAT - EDGE + r].astype(BF)


def pair_shift(low, high, axis):
    peers = lax.axis_size(axis)
    up = [(i, (i + 1) % peers) for i in range(peers)]
    down = [(j, i) for i, j in up]
    return lax.ppermute(high, axis, up), lax.ppermute(low, axis, down)


def kernel_params(limit):
    return pltpu.CompilerParams(vmem_limit_bytes=limit * 1024 * 1024)


def forward_call(first, count, *operands):
    whole = len(operands) - 7
    return pl.pallas_call(
        functools.partial(forward_kernel, first, count),
        out_shape=[
            sds((HIGH0, COLS, SUBL, HID), BF),
            sds((TAPE, EXP), BF),
            sds((TAPE, HID), BF),
            sds((TAPE, LANES), F32),
        ],
        in_specs=[vmem()] * 7 + [anywhere()] * whole,
        out_specs=[anywhere()] * 4,
        scratch_shapes=[
            pltpu.VMEM((count + 2, COLS, SUBL, HID), BF),
            pltpu.VMEM((2, WIDE, LANES), F32),
            pltpu.VMEM((9, SUBL, HID), BF),
            pltpu.VMEM((HID, LANES), BF),
            pltpu.VMEM((RF * WIDE, EXP), BF),
            pltpu.VMEM((3, RF * WIDE, EXP), BF),
            pltpu.VMEM((3, RF * WIDE, HID), BF),
            pltpu.VMEM((3, RF * WIDE, LANES), F32),
            pltpu.VMEM((3, RF, COLS, SUBL, HID), BF),
            pltpu.SemaphoreType.DMA((3, 4)),
        ],
        input_output_aliases={7 + k: k for k in range(whole)},
        compiler_params=kernel_params(16),
        cost_estimate=pl.CostEstimate(
            flops=MLP * count * 3, bytes_accessed=TAPE * EXP * 2, transcendentals=0
        ),
        name="forward_zero",
    )(*operands)


def main_call(channels, levels, *operands):
    return pl.pallas_call(
        functools.partial(main_kernel, levels),
        out_shape=sds((channels * LAT, LON), F32),
        in_specs=[vmem()] * 15,
        out_specs=vmem(),
        scratch_shapes=[
            pltpu.VMEM((3, 9, SUBL, HID), BF),
            pltpu.VMEM((HID, LANES), BF),
            pltpu.VMEM((2 * max(RM, RE), WIDE, LANES), F32),
            pltpu.VMEM((max(RM, RB) * WIDE, EXP), BF),
            pltpu.VMEM((RM * WIDE, EXP), BF),
            pltpu.VMEM((HIGH1, WIDE, levels), BF),
            pltpu.VMEM((HIGH1, COLS, SUBL, HID), BF),
            pltpu.VMEM((HIGH2, COLS, SUBL, HID), BF),
            pltpu.VMEM((HIGH2, COLS, SUBL, HID), BF),
            pltpu.VMEM((2, channels * LAT, LANES), F32),
        ],
        compiler_params=kernel_params(24),
        cost_estimate=pl.CostEstimate(
            flops=MLP * (2 * HIGH1 + HIGH2), bytes_accessed=TAPE * EXP * 2, transcendentals=0
        ),
        name="forward_one_and_adjoint",
    )(*operands)


def body(
    state, enc_weight, kernels, gains, up_weight, down_weight, dec_weight,
    obs_values, obs_cells, obs_depth,
):
    channels = state.shape[0]
    levels = dec_weight.shape[1]
    owners, slots = obs_cells.shape[1:]

    edges = lax.optimization_barrier((state[:, :HALO], state[:, LAT - HALO :], obs_cells))
    top, bottom = pair_shift(edges[0], edges[1], "lat")

    packed = pl.pallas_call(
        pack_observations,
        out_shape=sds((owners, 8, LANES), BF),
        in_specs=[vmem()] * 3,
        out_specs=vmem(),
        scratch_shapes=[pltpu.VMEM((8 * LANES, LANES), F32)] * 2,
        compiler_params=kernel_params(16),
        name="pack_observations",
    )(
        obs_values[0].transpose(1, 2, 0).reshape(slots * levels, owners),
        edges[2][0].T,
        obs_depth[0].T,
    )
    table = lax.all_to_all(packed, ("lat", "lon"), split_axis=0, concat_axis=0, tiled=True)

    band = lax.axis_index("lat")
    top = jnp.where(band > 0, top, 0)
    bottom = jnp.where(band < lax.axis_size("lat") - 1, bottom, 0)
    tall = jnp.concatenate([top, state, bottom], axis=1)
    main = lax.dot_general(
        tall, enc_weight, (((0,), (0,)), ((), ())), preferred_element_type=F32
    ).astype(BF)
    left, right = pair_shift(main[:, :SIDE], main[:, LON - SIDE :], "lon")

    field, f_top, f_bottom, f_left, f_right = pl.pallas_call(
        functools.partial(place_observations, slots, levels),
        out_shape=[
            sds((LAT, LON, 2 * LANES), F32),
            sds((EDGE, LON, 2 * LANES), BF),
            sds((EDGE, LON, 2 * LANES), BF),
            sds((LAT, SIDE, 2 * LANES), BF),
            sds((LAT, SIDE, 2 * LANES), BF),
        ],
        in_specs=[vmem()],
        out_specs=[vmem()] * 5,
        scratch_shapes=[
            pltpu.VMEM((8 * LANES, LANES), F32),
            pltpu.VMEM((LANES, 8 * LANES), F32),
            pltpu.VMEM((LON, slots * LANES), BF),
            pltpu.VMEM((8, slots * LANES), F32),
            pltpu.VMEM((slots * LANES, 2 * LANES), BF),
        ],
        compiler_params=kernel_params(24),
        cost_estimate=pl.CostEstimate(
            flops=2 * LAT * LON * slots * LANES * 256, bytes_accessed=2**22, transcendentals=0
        ),
        name="place_observations",
    )(table)

    west, east = pair_shift(f_left, f_right, "lon")
    first_rows = 10
    main, f_left = lax.optimization_barrier((main, f_left))
    part_a = forward_call(
        0, first_rows, left, main, right, kernels, gains, up_weight, down_weight
    )
    west, east, main, *part_a = lax.optimization_barrier((west, east, main, *part_a))
    low = jnp.concatenate([west[:EDGE], f_top, east[:EDGE]], axis=1)
    high = jnp.concatenate([west[LAT - EDGE :], f_bottom, east[LAT - EDGE :]], axis=1)
    above, below = pair_shift(low, high, "lat")
    main, low = lax.optimization_barrier((main, low))
    forward = forward_call(
        first_rows, HIGH0 - first_rows, left, main, right, kernels, gains, up_weight, down_weight,
        *part_a,
    )

    gradient = main_call(
        channels, levels, above, below, west, field, east, kernels, gains, up_weight,
        down_weight, dec_weight, enc_weight, *forward,
    )
    return gradient.reshape(channels, LAT, LON)


def solution(mesh):
    in_specs = (
        P(None, "lat", "lon"),
        P(),
        P(),
        P(),
        P(),
        P(),
        P(),
        P(("lat", "lon"), None, None, None),
        P(("lat", "lon"), None, None),
        P(("lat", "lon"), None, None),
    )
    out_specs = P(None, "lat", "lon")
    return jax.shard_map(body, mesh=mesh, in_specs=in_specs, out_specs=out_specs, check_vma=False)
```

```python
import functools
import math

import jax
import jax.numpy as jnp
from jax import lax
from jax.experimental import pallas as pl
from jax.experimental.pallas import tpu as pltpu
from jax.sharding import PartitionSpec as P

EPSILON = 1e-06
SQRT_TWO_PI = math.sqrt(2.0 / math.pi)
CUBIC = SQRT_TWO_PI * 0.044715
BF = jnp.bfloat16
F32 = jnp.float32

LAT = 16
LON = 256
HID = 256
EXP = 1024
LANES = 128
SIDE = 8
WIDE = LON + 2 * SIDE
SUBL = 16
COLS = WIDE // SUBL
HALO = 4
CHUNK = 256
HIGH0 = LAT + 2 * HALO - 2
HIGH1 = HIGH0 - 2
HIGH2 = HIGH1 - 2
TAPE = HIGH2 * WIDE
MLP = 2 * WIDE * HID * EXP * 2
RF = 2
RM = 4
RB = 6
RE = 4
EDGE = 2


def sds(shape, dtype):
    return jax.ShapeDtypeStruct(shape, dtype)


def vmem():
    return pl.BlockSpec(memory_space=pltpu.VMEM)


def anywhere():
    return pl.BlockSpec(memory_space=pl.ANY)


def turn(value, shift):
    return pltpu.roll(value.astype(F32), shift, 0).astype(value.dtype)


def convolve(rows, taps):
    out = []
    for r in range(len(rows) - 2):
        part = [
            taps[e] * rows[r] + taps[3 + e] * rows[r + 1] + taps[6 + e] * rows[r + 2]
            for e in range(3)
        ]
        first = turn(part[0][COLS - 1], 1)
        last = turn(part[2][0], SUBL - 1)
        west = jnp.concatenate([first[None], part[0][:-1]], axis=0)
        east = jnp.concatenate([part[2][1:], last[None]], axis=0)
        out.append(part[1] + west + east)
    return out


def fill_taps(tap_ref, kernel_ref, b, flip):
    for a in range(3):
        for e in range(3):
            row = kernel_ref[b, a, e : e + 1, :]
            at = (2 - a) * 3 + 2 - e if flip else a * 3 + e
            tap_ref[at] = jnp.broadcast_to(row, (SUBL, HID)).astype(BF)


def taps_of(tap_ref):
    return [tap_ref[t] for t in range(9)]


def flat(rows):
    return jnp.concatenate([row.reshape(WIDE, HID) for row in rows], axis=0)


def twice(value):
    return jnp.concatenate([value, value], axis=1)


def gelu_pair(pre):
    v = pre.astype(BF)
    u = v * v
    t = jnp.tanh(v * (u * CUBIC + SQRT_TWO_PI))
    w = 1.0 + t
    return v * w, w * (1.0 + (v * (u * (3.0 * CUBIC) + SQRT_TWO_PI)) * (1.0 - t))


def times_transposed(left, right):
    return lax.dot_general(left, right, (((1,), (1,)), ((), ())), preferred_element_type=F32)


def normalize(spatial, mean_ref):
    square = (spatial * spatial).astype(BF)
    mean = jnp.dot(square, mean_ref[...], preferred_element_type=F32)
    inv = lax.rsqrt(mean + EPSILON)
    return inv, spatial * twice(inv.astype(BF))


def forward(b, hat, gain_ref, up_ref, down_ref, act_ref, slope_ref):
    normed = hat * gain_ref[b : b + 1, :].astype(BF)
    for j in range(EXP // CHUNK):
        cut = slice(j * CHUNK, (j + 1) * CHUNK)
        pre = jnp.dot(normed, up_ref[b, :, cut], preferred_element_type=F32)
        act, slope = gelu_pair(pre)
        act_ref[:, cut] = act
        slope_ref[:, cut] = slope
    return 0.5 * jnp.dot(act_ref[...], down_ref[b], preferred_element_type=F32)


def backward(b, grad_s, hat, inv, gain_ref, up_ref, down_ref, act_ref, slope_ref, mean_ref):
    for j in range(EXP // CHUNK):
        cut = slice(j * CHUNK, (j + 1) * CHUNK)
        grad_g = times_transposed(grad_s, down_ref[b, cut, :])
        act_ref[:, cut] = grad_g.astype(BF) * slope_ref[:, cut]
    weighted = times_transposed(act_ref[...], up_ref[b]) * (0.5 * gain_ref[b : b + 1, :])
    weighted = weighted.astype(BF)
    projection = jnp.dot(weighted * hat, mean_ref[...], preferred_element_type=F32)
    return twice(inv.astype(BF)) * (weighted - hat * twice(projection.astype(BF)))


def row_mask(first):
    row = lax.axis_index("lat") * LAT + first
    ok = jnp.logical_and(row >= 0, row < lax.axis_size("lat") * LAT)
    return jnp.where(ok, 1.0, 0.0).astype(F32)


def store_rows(ref, base, value, first=None):
    for r in range(value.shape[0] // WIDE):
        part = value[r * WIDE : (r + 1) * WIDE]
        if first is not None:
            part = part * row_mask(first + r).astype(part.dtype)
        ref[base + r] = part.astype(BF).reshape(COLS, SUBL, HID)


def from_natural(ref):
    return jnp.concatenate([ref[pl.ds(t, SUBL, stride=COLS), :] for t in range(COLS)], axis=0)


def forward_kernel(
    first, count,
    left_ref, main_ref, right_ref, kernel_ref, gain_ref, up_ref, down_ref, *rest
):
    (
        out_all, tape_all, hat_all, inv_all,
        hidden, natural, taps, mean_ref, act, slope, hats, invs, outs, sem,
    ) = rest[-14:]
    fill_taps(taps, kernel_ref, 0, False)
    mean_ref[...] = jnp.full((HID, LANES), 1.0 / HID, BF)

    @pl.loop(0, count + 2)
    def _(i):
        for half in range(2):
            lanes = slice(half * LANES, (half + 1) * LANES)
            natural[half, 0:SIDE, :] = left_ref[first + i, :, lanes].astype(F32)
            natural[half, SIDE : SIDE + LON, :] = main_ref[first + i, :, lanes].astype(F32)
            natural[half, SIDE + LON : WIDE, :] = right_ref[first + i, :, lanes].astype(F32)
            row = from_natural(natural.at[half]).astype(BF)
            hidden[i, :, :, lanes] = row.reshape(COLS, SUBL, LANES)

    steps = count // RF
    taped = max(1 - first // RF, 0)
    ends = min((HIGH0 - first) // RF - 1, steps)

    def kept(i, slot):
        at = pl.ds(first + i * RF, RF)
        return [pltpu.make_async_copy(outs.at[slot], out_all.at[at], sem.at[slot, 3])]

    def copies(i, slot):
        at = pl.ds(pl.multiple_of((first // RF + i - 1) * RF * WIDE, 16), RF * WIDE)
        return [
            pltpu.make_async_copy(slope.at[slot], tape_all.at[at], sem.at[slot, 0]),
            pltpu.make_async_copy(hats.at[slot], hat_all.at[at], sem.at[slot, 1]),
            pltpu.make_async_copy(invs.at[slot], inv_all.at[at], sem.at[slot, 2]),
        ]

    @pl.loop(0, steps)
    def _(i):
        slot = lax.rem(i, 3)

        @pl.when(i >= 3)
        def _():
            for copy in kept(i - 3, slot):
                copy.wait()

        @pl.when(i >= taped + 3)
        def _():
            for copy in copies(i - 3, slot):
                copy.wait()

        rows = [hidden[i * RF + a] for a in range(RF + 2)]
        inv, hat = normalize(flat(convolve(rows, taps_of(taps))), mean_ref)
        hats[slot] = hat
        invs[slot] = inv
        branch = forward(0, hat, gain_ref, up_ref, down_ref, act, slope.at[slot])
        total = flat(rows[1:-1]).astype(F32) + branch
        store_rows(outs.at[slot], 0, total, first + i * RF + 1 - HALO)
        for copy in kept(i, slot):
            copy.start()

        @pl.when(jnp.logical_and(i >= taped, i < ends))
        def _():
            for copy in copies(i, slot):
                copy.start()

    for i in range(steps - 3, steps):
        for copy in kept(i, i % 3):
            copy.wait()
    for i in range(max(taped, steps - 3), ends):
        for copy in copies(i, i % 3):
            copy.wait()


def main_kernel(
    levels,
    above_ref, below_ref, left_ref, main_ref, right_ref, kernel_ref, gain_ref, up_ref, down_ref,
    dec_ref, enc_ref, hidden, tape, hats, invs,
    out_ref,
    taps, mean_ref, natural, act, slope, adjoint, grad_d1, grad_d0, grad1, gathered,
):
    mean_ref[...] = jnp.full((HID, LANES), 1.0 / HID, BF)
    fill_taps(taps.at[0], kernel_ref, 1, False)
    fill_taps(taps.at[1], kernel_ref, 1, True)
    fill_taps(taps.at[2], kernel_ref, 0, True)
    last = HIGH1 // RM - 1

    @pl.loop(0, HIGH1 // RM)
    def _(i):
        for r in range(RM):
            inner = True
            for edge, ref, at in ((0, above_ref, r), (last, below_ref, r - RM + EDGE)):
                if 0 <= at < EDGE:
                    inner = jnp.logical_and(inner, i != edge)

                    @pl.when(i == edge)
                    def _():
                        for half in range(2):
                            lanes = slice(half * LANES, (half + 1) * LANES)
                            row = ref[at, :, lanes].astype(F32)
                            natural[2 * r + half] = row * row_mask(i * RM + r - EDGE)

            @pl.when(inner)
            def _():
                row = i * RM + r - EDGE
                for half in range(2):
                    lanes = slice(half * LANES, (half + 1) * LANES)
                    place = natural.at[2 * r + half]
                    place[0:SIDE, :] = left_ref[row, :, lanes].astype(F32)
                    place[SIDE : SIDE + LON, :] = main_ref[row, :, lanes]
                    place[SIDE + LON : WIDE, :] = right_ref[row, :, lanes].astype(F32)

        rows = [hidden[i * RM + a] for a in range(RM + 2)]
        inv, hat = normalize(flat(convolve(rows, taps_of(taps.at[0]))), mean_ref)
        branch = forward(1, hat, gain_ref, up_ref, down_ref, act.at[: RM * WIDE], slope)
        final = (flat(rows[1:-1]).astype(F32) + branch).astype(BF)
        model = jnp.dot(final, dec_ref[...], preferred_element_type=F32)
        sums = jnp.concatenate([from_natural(natural.at[2 * r]) for r in range(RM)], axis=0)
        counts = jnp.concatenate([from_natural(natural.at[2 * r + 1]) for r in range(RM)], axis=0)
        adj = (counts[:, :levels] * model - sums[:, :levels]).astype(BF)
        for r in range(RM):
            adjoint[i * RM + r] = adj[r * WIDE : (r + 1) * WIDE]
        grad_s = times_transposed(adj, dec_ref[...]).astype(BF)
        grad_d = backward(
            1, grad_s, hat, inv, gain_ref, up_ref, down_ref, act.at[: RM * WIDE], slope, mean_ref
        )
        store_rows(grad_d1, i * RM, grad_d)

    @pl.loop(0, HIGH2 // RB)
    def _(i):
        rows = [grad_d1[i * RB + a] for a in range(RB + 2)]
        adj = jnp.concatenate([adjoint[i * RB + 1 + r] for r in range(RB)], axis=0)
        grad = times_transposed(adj, dec_ref[...])
        grad = grad + flat(convolve(rows, taps_of(taps.at[1]))).astype(F32)
        grad_s = grad.astype(BF)
        store_rows(grad1, i * RB, grad_s)
        at = pl.ds(pl.multiple_of(i * RB * WIDE, 16), RB * WIDE)
        grad_d = backward(
            0, grad_s, hats[at], invs[at], gain_ref, up_ref, down_ref, act.at[: RB * WIDE], tape.at[at],
            mean_ref
        )
        store_rows(grad_d0, i * RB, grad_d, i * RB - 1)

    @pl.loop(0, LAT // RE)
    def _(i):
        rows = [grad_d0[i * RE + a] for a in range(RE + 2)]
        conv = convolve(rows, taps_of(taps.at[2]))
        for r in range(RE):
            total = conv[r].astype(F32) + grad1[i * RE + 1 + r].astype(F32)
            halves = []
            for half in range(2):
                place = natural.at[2 * r + half]
                for t in range(COLS):
                    place[pl.ds(t, SUBL, stride=COLS), :] = total[
                        t, :, half * LANES : (half + 1) * LANES
                    ]
                halves.append(place[SIDE : SIDE + LON, :].astype(BF))
            result = times_transposed(enc_ref[...], jnp.concatenate(halves, axis=1))
            for half in range(2):
                gathered[half, pl.ds(i * RE + r, enc_ref.shape[0], stride=LAT), :] = result[
                    :, half * LANES : (half + 1) * LANES
                ]

    for half in range(2):
        out_ref[:, half * LANES : (half + 1) * LANES] = gathered[half]


def pack_observations(value_ref, cell_ref, depth_ref, out_ref, flipped, spread):
    used = value_ref.shape[0]
    slots = cell_ref.shape[0]
    cells = cell_ref[...]
    row = lax.shift_right_logical(cells, LON.bit_length() - 1)
    flipped[:used] = value_ref[...]
    flipped[used : used + slots] = row.astype(F32)
    flipped[used + slots : used + 2 * slots] = (cells - row * LON).astype(F32)
    flipped[used + 2 * slots : used + 3 * slots] = depth_ref[...].astype(F32)
    flipped[used + 3 * slots :] = jnp.zeros_like(flipped[used + 3 * slots :])
    for k in range(8):
        block = jnp.transpose(flipped[k * LANES : (k + 1) * LANES, :])
        spread[pl.ds(k, LANES, stride=8), :] = block
    out_ref[...] = spread[...].reshape(LANES, 8, LANES).astype(BF)


def place_observations(
    slots, levels, table_ref,
    field_ref, top_ref, bottom_ref, left_ref, right_ref,
    spread, wide, hot, row_ref, values,
):
    spread[...] = table_ref[...].astype(F32).reshape(LANES * 8, LANES)
    for k in range(8):
        wide[:, k * LANES : (k + 1) * LANES] = spread[pl.ds(k, LANES, stride=8), :]
    used = slots * levels
    base = used // LANES * LANES
    tags = jnp.transpose(wide[:, base : base + LANES])
    lane = lax.broadcasted_iota(jnp.int32, (LANES, levels), 1).astype(F32)
    column = lax.broadcasted_iota(jnp.int32, (LON, LANES), 0).astype(F32)
    at = used - base
    values[...] = jnp.zeros_like(values)
    for q in range(slots):
        part = slice(q * LANES, (q + 1) * LANES)
        depth = wide[:, used + 2 * slots + q : used + 2 * slots + q + 1]
        mask = jnp.where(lane < depth, 1.0, 0.0)
        values[part, :levels] = (wide[:, q * levels : (q + 1) * levels] * mask).astype(BF)
        values[part, LANES : LANES + levels] = mask.astype(BF)
        row_ref[0:1, part] = tags[at + q : at + q + 1, :]
        where = tags[at + slots + q : at + slots + q + 1, :]
        hot[:, part] = jnp.where(column == where, 1.0, 0.0).astype(BF)

    group = 8

    @pl.loop(0, LAT // group)
    def _(i):
        here = [
            jnp.where(row_ref[0:1, :] == (i * group + r).astype(F32), 1.0, 0.0).astype(BF)
            for r in range(group)
        ]
        left = jnp.concatenate([hot[...] * keep for keep in here], axis=0)
        total = jnp.dot(left, values[...], preferred_element_type=F32)
        for r in range(group):
            row = total[r * LON : (r + 1) * LON]
            field_ref[i * group + r] = row
            left_ref[i * group + r] = row[:SIDE].astype(BF)
            right_ref[i * group + r] = row[LON - SIDE :].astype(BF)

    for r in range(EDGE):
        top_ref[r] = field_ref[r].astype(BF)
        bottom_ref[r] = field_ref[LAT - EDGE + r].astype(BF)


def pair_shift(low, high, axis):
    peers = lax.axis_size(axis)
    up = [(i, (i + 1) % peers) for i in range(peers)]
    down = [(j, i) for i, j in up]
    return lax.ppermute(high, axis, up), lax.ppermute(low, axis, down)


def kernel_params(limit):
    return pltpu.CompilerParams(vmem_limit_bytes=limit * 1024 * 1024)


def forward_call(first, count, *operands):
    whole = len(operands) - 7
    return pl.pallas_call(
        functools.partial(forward_kernel, first, count),
        out_shape=[
            sds((HIGH0, COLS, SUBL, HID), BF),
            sds((TAPE, EXP), BF),
            sds((TAPE, HID), BF),
            sds((TAPE, LANES), F32),
        ],
        in_specs=[vmem()] * 7 + [anywhere()] * whole,
        out_specs=[anywhere()] * 4,
        scratch_shapes=[
            pltpu.VMEM((count + 2, COLS, SUBL, HID), BF),
            pltpu.VMEM((2, WIDE, LANES), F32),
            pltpu.VMEM((9, SUBL, HID), BF),
            pltpu.VMEM((HID, LANES), BF),
            pltpu.VMEM((RF * WIDE, EXP), BF),
            pltpu.VMEM((3, RF * WIDE, EXP), BF),
            pltpu.VMEM((3, RF * WIDE, HID), BF),
            pltpu.VMEM((3, RF * WIDE, LANES), F32),
            pltpu.VMEM((3, RF, COLS, SUBL, HID), BF),
            pltpu.SemaphoreType.DMA((3, 4)),
        ],
        input_output_aliases={7 + k: k for k in range(whole)},
        compiler_params=kernel_params(16),
        cost_estimate=pl.CostEstimate(
            flops=MLP * count * 3, bytes_accessed=TAPE * EXP * 2, transcendentals=0
        ),
        name="forward_zero",
    )(*operands)


def main_call(channels, levels, *operands):
    return pl.pallas_call(
        functools.partial(main_kernel, levels),
        out_shape=sds((channels * LAT, LON), F32),
        in_specs=[vmem()] * 15,
        out_specs=vmem(),
        scratch_shapes=[
            pltpu.VMEM((3, 9, SUBL, HID), BF),
            pltpu.VMEM((HID, LANES), BF),
            pltpu.VMEM((2 * max(RM, RE), WIDE, LANES), F32),
            pltpu.VMEM((max(RM, RB) * WIDE, EXP), BF),
            pltpu.VMEM((RM * WIDE, EXP), BF),
            pltpu.VMEM((HIGH1, WIDE, levels), BF),
            pltpu.VMEM((HIGH1, COLS, SUBL, HID), BF),
            pltpu.VMEM((HIGH2, COLS, SUBL, HID), BF),
            pltpu.VMEM((HIGH2, COLS, SUBL, HID), BF),
            pltpu.VMEM((2, channels * LAT, LANES), F32),
        ],
        compiler_params=kernel_params(24),
        cost_estimate=pl.CostEstimate(
            flops=MLP * (2 * HIGH1 + HIGH2), bytes_accessed=TAPE * EXP * 2, transcendentals=0
        ),
        name="forward_one_and_adjoint",
    )(*operands)


def body(
    state, enc_weight, kernels, gains, up_weight, down_weight, dec_weight,
    obs_values, obs_cells, obs_depth,
):
    channels = state.shape[0]
    levels = dec_weight.shape[1]
    owners, slots = obs_cells.shape[1:]

    edges = lax.optimization_barrier((state[:, :HALO], state[:, LAT - HALO :], obs_cells))
    top, bottom = pair_shift(edges[0], edges[1], "lat")

    packed = pl.pallas_call(
        pack_observations,
        out_shape=sds((owners, 8, LANES), BF),
        in_specs=[vmem()] * 3,
        out_specs=vmem(),
        scratch_shapes=[pltpu.VMEM((8 * LANES, LANES), F32)] * 2,
        compiler_params=kernel_params(16),
        name="pack_observations",
    )(
        obs_values[0].transpose(1, 2, 0).reshape(slots * levels, owners),
        edges[2][0].T,
        obs_depth[0].T,
    )
    table = lax.all_to_all(packed, ("lat", "lon"), split_axis=0, concat_axis=0, tiled=True)

    band = lax.axis_index("lat")
    top = jnp.where(band > 0, top, 0)
    bottom = jnp.where(band < lax.axis_size("lat") - 1, bottom, 0)
    tall = jnp.concatenate([top, state, bottom], axis=1)
    main = lax.dot_general(
        tall, enc_weight, (((0,), (0,)), ((), ())), preferred_element_type=F32
    ).astype(BF)
    left, right = pair_shift(main[:, :SIDE], main[:, LON - SIDE :], "lon")

    field, f_top, f_bottom, f_left, f_right = pl.pallas_call(
        functools.partial(place_observations, slots, levels),
        out_shape=[
            sds((LAT, LON, 2 * LANES), F32),
            sds((EDGE, LON, 2 * LANES), BF),
            sds((EDGE, LON, 2 * LANES), BF),
            sds((LAT, SIDE, 2 * LANES), BF),
            sds((LAT, SIDE, 2 * LANES), BF),
        ],
        in_specs=[vmem()],
        out_specs=[vmem()] * 5,
        scratch_shapes=[
            pltpu.VMEM((8 * LANES, LANES), F32),
            pltpu.VMEM((LANES, 8 * LANES), F32),
            pltpu.VMEM((LON, slots * LANES), BF),
            pltpu.VMEM((8, slots * LANES), F32),
            pltpu.VMEM((slots * LANES, 2 * LANES), BF),
        ],
        compiler_params=kernel_params(24),
        cost_estimate=pl.CostEstimate(
            flops=2 * LAT * LON * slots * LANES * 256, bytes_accessed=2**22, transcendentals=0
        ),
        name="place_observations",
    )(table)

    west, east = pair_shift(f_left, f_right, "lon")
    first_rows = 6
    main, f_left = lax.optimization_barrier((main, f_left))
    part_a = forward_call(
        0, first_rows, left, main, right, kernels, gains, up_weight, down_weight
    )
    west, east, main, *part_a = lax.optimization_barrier((west, east, main, *part_a))
    low = jnp.concatenate([west[:EDGE], f_top, east[:EDGE]], axis=1)
    high = jnp.concatenate([west[LAT - EDGE :], f_bottom, east[LAT - EDGE :]], axis=1)
    above, below = pair_shift(low, high, "lat")
    main, low = lax.optimization_barrier((main, low))
    forward = forward_call(
        first_rows, HIGH0 - first_rows, left, main, right, kernels, gains, up_weight, down_weight,
        *part_a,
    )

    gradient = main_call(
        channels, levels, above, below, west, field, east, kernels, gains, up_weight,
        down_weight, dec_weight, enc_weight, *forward,
    )
    return gradient.reshape(channels, LAT, LON)


def solution(mesh):
    in_specs = (
        P(None, "lat", "lon"),
        P(),
        P(),
        P(),
        P(),
        P(),
        P(),
        P(("lat", "lon"), None, None, None),
        P(("lat", "lon"), None, None),
        P(("lat", "lon"), None, None),
    )
    out_specs = P(None, "lat", "lon")
    return jax.shard_map(body, mesh=mesh, in_specs=in_specs, out_specs=out_specs, check_vma=False)
```
